256 devices in a mesh: rep: 4 (over z_lo, core), fsdp: 64 (over x, z_hi, y).
Axes of the slice: x: 4, y: 4, z: 8 (z_hi: 4, z_lo: 2; z = z_hi * 2 + z_lo), core: 2. Of those that a mesh axis runs over, the one named last changes fastest.
Arguments:
- normed: bfloat16 [98304, 4608], P(('rep', 'fsdp')), may hold values from -24 to 24
- key_grad: bfloat16 [98304, 1024], P(('rep', 'fsdp')), may hold values from -6 to 6
- master: float32 [4, 4608, 1024], P('rep', 'fsdp'), may hold values from -6 to 6
- first_moment: float32 [4, 4608, 1024], P('rep', 'fsdp'), may hold values from -6 to 6
- second_moment: float32 [4, 4608, 1024], P('rep', 'fsdp'), may hold values from 0.1 to 10
- anchor: float32 [4608, 1024], P('fsdp'), may hold values from -6 to 6
- momentum: float32 [4608, 1024], P('fsdp'), may hold values from -6 to 6
- inner_step: int32 [1], replicated, may hold values from 1 to 6
Outputs:
- keys: bfloat16 [98304, 1024], P(('rep', 'fsdp'))
- input_grad: bfloat16 [98304, 4608], P(('rep', 'fsdp'))
- merged: float32 [4, 4608, 1024], P('rep', 'fsdp')
- new_first: float32 [4, 4608, 1024], P('rep', 'fsdp')
- new_second: float32 [4, 4608, 1024], P('rep', 'fsdp')
- new_anchor: float32 [4608, 1024], P('fsdp')
- new_momentum: float32 [4608, 1024], P('fsdp')
The draws below stay inside these ranges and needn't reach their ends.
Inputs may be any that keep to these rules, and one draw needn't show every extreme that they name: `inner_step`: the 1-based count of inner steps taken by the inner optimizer.
All inputs are finite; a program needn't handle non-finite values.
Results may differ from the reference program's by a relative error of at most 0.0049.
Values may be sent and summed in bfloat16 or wider, within the bound.
A program may use at most 128 MiB of HBM per device.

```python
import math
import jax
import jax.numpy as jnp
from jax import lax

D = 4608
TOK_DEV = 384
KD = 1024
TOKENS = 98304
N_REP = 4
N_FSDP = 64


def with_spikes(result, own_key, source, target, shards_of, factor):
    def block_of(axis_at):
        return (jnp.arange(result.shape[axis_at]) // (result.shape[axis_at] // shards_of)).reshape((-1,) + (1,) * (result.ndim - 1 - axis_at))

    first = jax.random.permutation(own_key, shards_of)[block_of(target)]
    far = (block_of(target) + shards_of // 2) % shards_of
    return jnp.where((block_of(source) == first) | (block_of(source) == far), factor * result, result)


def level_of(rng, dims, pieces, least, high):
    loudness = 1.0
    for axis_at, parts in pieces:
        draws = jax.random.uniform(jax.random.fold_in(jax.random.fold_in(rng, 6), axis_at), (parts,), jnp.float32, least / len(pieces), high / len(pieces))
        loudness = loudness * jnp.repeat(jnp.exp(draws), dims[axis_at] // parts).reshape((-1,) + (1,) * (len(dims) - 1 - axis_at))
    return loudness


def scatter_about(own_key, extent, spread, limit, split=(), held_as=jnp.bfloat16):
    entries = jax.random.normal(own_key, extent, jnp.float32) * spread
    if len(split) > 0:
        entries = level_of(own_key, extent, split, -0.22, 0.18) * entries
    return jnp.clip(entries, min=-limit, max=limit).astype(held_as)


def noise_with(stream_key, shape, deviation, most, pieces, heavy, held_as=jnp.bfloat16):
    entries = deviation * jax.random.normal(stream_key, shape, jnp.float32)
    if pieces:
        entries = entries * level_of(stream_key, shape, pieces, -0.22, 0.18)
    return jnp.clip(with_spikes(entries, jax.random.fold_in(stream_key, 3), *heavy), -most, most).astype(held_as)


def setup_inputs(seed: int = 0) -> dict:
    streams_of = jax.random.split(jax.random.key(seed), 9)
    normed = noise_with(streams_of[0], (TOKENS, D), 1.0, 24.0, ((0, 256),), (0, 1, 256, 6.0))
    key_grad = scatter_about(streams_of[1], (TOKENS, KD), 1.0, 6.0, ((0, 256),))
    master = scatter_about(streams_of[2], (N_REP, D, KD), 1.0, 6.0, ((0, 4), (1, 64)), jnp.float32)
    first_moment = scatter_about(streams_of[3], (N_REP, D, KD), 1.0, 6.0, ((0, 4), (1, 64)), jnp.float32)
    second_moment = jnp.clip(jnp.exp(math.log(10.0) - 4.6051702 * jax.random.uniform(streams_of[4], (N_REP, D, KD), jnp.float32) ** level_of(streams_of[4], (N_REP, D, KD), ((0, 4), (1, 64)), -0.2, 0.2)), 0.1, 10.0)
    anchor = scatter_about(streams_of[5], (D, KD), 1.0, 6.0, ((0, 64),), jnp.float32)
    momentum = scatter_about(streams_of[6], (D, KD), 0.5, 6.0, ((0, 64),), jnp.float32)
    inner_step = jax.random.randint(streams_of[7], (1,), 1, 7).astype(jnp.int32)
    return {"normed": normed, "key_grad": key_grad, "master": master, "first_moment": first_moment, "second_moment": second_moment, "anchor": anchor, "momentum": momentum, "inner_step": inner_step}


beta_first = 0.9
beta_second = 0.95
inner_rate = 0.1
weight_decay = 0.1
epsilon = 1e-08
outer_rate = 0.7
outer_mu = 0.9
mix_weight = 0.5

def reference(normed, key_grad, master, first_moment, second_moment, anchor, momentum, inner_step):
    scale = D ** (-0.5)
    count = inner_step[0].astype(jnp.float32)
    fix_first = 1.0 - jnp.power(jnp.float32(beta_first), count)
    fix_second = 1.0 - jnp.power(jnp.float32(beta_second), count)
    delta_sum = jnp.zeros((D, KD), jnp.float32)
    for index in range(N_REP):
        delta_sum = delta_sum + (anchor - master[index])
    outer_grad = delta_sum / N_REP
    new_momentum = outer_mu * momentum + outer_grad
    new_anchor = anchor - outer_rate * (outer_grad + outer_mu * new_momentum)
    span = TOK_DEV * N_FSDP
    key_parts, grad_parts, merged_parts, first_parts, second_parts = ([], [], [], [], [])
    for index in range(N_REP):
        inputs = normed[index * span:(index + 1) * span]
        cotangent = key_grad[index * span:(index + 1) * span]
        weight_half = master[index].astype(jnp.bfloat16)
        key_parts.append((jnp.dot(inputs, weight_half, preferred_element_type=jnp.float32) * scale).astype(jnp.bfloat16))
        grad_parts.append((jnp.dot(cotangent, weight_half.T, preferred_element_type=jnp.float32) * scale).astype(jnp.bfloat16))
        gradient = lax.dot_general(inputs, cotangent, (((0,), (0,)), ((), ())), preferred_element_type=jnp.float32) * scale
        first_new = beta_first * first_moment[index] + (1.0 - beta_first) * gradient
        second_new = beta_second * second_moment[index] + (1.0 - beta_second) * gradient * gradient
        direction = first_new / fix_first / (jnp.sqrt(second_new / fix_second) + epsilon)
        stepped = master[index] - inner_rate * (direction + weight_decay * master[index])
        merged_parts.append(mix_weight * stepped + (1.0 - mix_weight) * new_anchor)
        first_parts.append(first_new)
        second_parts.append(second_new)
    return (jnp.concatenate(key_parts, 0), jnp.concatenate(grad_parts, 0), jnp.stack(merged_parts), jnp.stack(first_parts), jnp.stack(second_parts), new_anchor, new_momentum)
```

```python
import jax
import jax.numpy as jnp
from jax import lax
from jax.experimental import pallas as pl
from jax.experimental.pallas import tpu as pltpu
from jax.sharding import PartitionSpec as P

beta_first = 0.9
beta_second = 0.95
inner_rate = 0.1
weight_decay = 0.1
epsilon = 1e-08
outer_rate = 0.7
outer_mu = 0.9
mix_weight = 0.5

MESH = pl.DeviceIdType.MESH
D, KD, TOK = 4608, 1024, 384
ROWS = 72
HALF = KD // 2
CHUNK = 4 * ROWS
HROWS = CHUNK // 2
BLOCK = 4 * CHUNK
TO_RIGHT = (2, 0)
TO_LEFT = (1, 3)
F32, BF16 = jnp.float32, jnp.bfloat16


def f32(v):
    return v.astype(F32)


def kernel(
    normed_hbm, kg_hbm, master_hbm, keys_hbm, ig_hbm, grad_hbm,
    xv, kgv, mv, keysv, igv, gradv,
    w, wnat, g, gnat, first_send, first_recv,
    r1, r1x, r2, r2x, third, r3,
    load_sem, store_sem,
    f_send, f_got, a2_send, a2_got, a2x_send, a2x_got,
    a3_send, a3_got, a3x_send, a3x_got,
    s1x_send, s1x_got, s1_send, s1_got,
    s2x_send, s2x_got, s2_send, s2_got, s3_send, s3_got,
):
    rep = lax.axis_index("rep")
    shard = lax.axis_index("fsdp")
    x, z, y = shard // 16, (shard // 4) % 4, shard % 4

    def dev(dx, dz, dy):
        return (rep, ((x + dx) % 4) * 16 + ((z + dz) % 4) * 4 + (y + dy) % 4)

    first_pos, last_pos = (x, y), (y, x)
    first_dev = (lambda d: dev(d, 0, 0), lambda d: dev(0, 0, d))
    last_dev = (first_dev[1], first_dev[0])

    def z_dev(d):
        return dev(0, d, 0)

    pending = []

    def send(src, dst, ssem, rsem, target):
        copy = pltpu.make_async_remote_copy(
            src_ref=src, dst_ref=dst, send_sem=ssem, recv_sem=rsem,
            device_id=target, device_id_type=MESH,
        )
        copy.start()
        pending.append(copy)

    def got(dst, ssem, rsem):
        pltpu.make_async_remote_copy(
            src_ref=dst, dst_ref=dst, send_sem=ssem, recv_sem=rsem,
            device_id=z_dev(1), device_id_type=MESH,
        ).wait_recv()

    loads = [
        pltpu.make_async_copy(master_hbm, mv, load_sem.at[0]),
        pltpu.make_async_copy(normed_hbm, xv, load_sem.at[1]),
        pltpu.make_async_copy(kg_hbm, kgv, load_sem.at[2]),
    ]
    for copy in loads:
        copy.start()

    barrier = pltpu.get_barrier_semaphore()
    peers = [first_dev[s](d) for s in (0, 1) for d in (1, 3, 2)] + [z_dev(1), z_dev(3)]
    for peer in peers:
        pl.semaphore_signal(barrier, inc=1, device_id=peer, device_id_type=MESH)
    pl.semaphore_wait(barrier, len(peers))

    loads[0].wait()
    for s in (0, 1):
        own = mv[:, s * HALF:(s + 1) * HALF]
        packed = jnp.concatenate([own[:, :HALF // 2], own[:, HALF // 2:]], axis=0).astype(BF16)
        first_send[s] = packed
        first_recv[s, first_pos[s]] = packed
        for d in (1, 3, 2):
            send(first_send.at[s], first_recv.at[s, first_pos[s]],
                 f_send.at[s, d], f_got.at[s, d], first_dev[s](d))

    def chunk_at(s, d, k):
        return ((last_pos[s] + d) % 4) * 4 + (z + k) % 4

    def send_relay(s):
        for n, k in enumerate(TO_RIGHT):
            send(g.at[s, chunk_at(s, 2, k)], r1x.at[s, 0, n],
                 s1x_send.at[s, 0, n], s1x_got.at[s, 0, n], last_dev[s](1))
        for n, k in enumerate(TO_LEFT):
            send(g.at[s, chunk_at(s, 2, k)], r1x.at[s, 1, n],
                 s1x_send.at[s, 1, n], s1x_got.at[s, 1, n], last_dev[s](3))

    def send_one(s, way, k):
        send(g.at[s, chunk_at(s, 1 if way == 0 else 3, k)], r1.at[s, way, k],
             s1_send.at[s, way, k], s1_got.at[s, way, k], last_dev[s](1 if way == 0 else 3))

    loads[1].wait()
    loads[2].wait()

    def tn(lhs, rhs):
        return lax.dot_general(lhs, rhs, (((0,), (0,)), ((), ())), preferred_element_type=F32)

    def grad_one(block):
        def step(i, _):
            at = pl.multiple_of(block * BLOCK + i * TOK, 128)
            part = tn(xv[:, pl.ds(at, TOK)], kgv[:, HALF:]).astype(BF16)
            flat = g.at[1, pl.ds(block * 4, 4)]
            for n in range(TOK // 96):
                row = i * TOK + n * 96
                flat[row // CHUNK, pl.ds(pl.multiple_of(row % CHUNK, 96), 96)] = part[n * 96:(n + 1) * 96]
            return 0
        lax.fori_loop(0, BLOCK // TOK, step, 0)

    grad_one((x + 2) % 4)
    send_relay(1)

    def grad_zero(i, _):
        at = pl.multiple_of(i * TOK, 128)
        gnat[pl.ds(at, TOK)] = tn(xv[:, pl.ds(at, TOK)], kgv[:, :HALF])
        return 0
    lax.fori_loop(0, D // TOK, grad_zero, 0)

    def pack(block):
        def step(k, _):
            for half in (0, 1):
                pieces = [
                    gnat[pl.ds(pl.multiple_of(a * BLOCK + k * CHUNK + block * ROWS, 8), ROWS)]
                    for a in (2 * half, 2 * half + 1)
                ]
                g[0, block * 4 + k, half * HROWS:(half + 1) * HROWS] = jnp.concatenate(pieces, axis=0).astype(BF16)
            return 0
        lax.fori_loop(0, 4, step, 0)

    pack((y + 2) % 4)
    send_relay(0)
    for d in (1, 3):
        grad_one((x + d) % 4)
        pack((y + d) % 4)
        for s in (1, 0):
            way = 0 if d == 1 else 1
            for k in (TO_LEFT if d == 1 else TO_RIGHT):
                send_one(s, way, k)
    grad_one(x)
    pack(y)

    def send_second(s, way, h):
        here = w.at[s, last_pos[s] * 4 + z, pl.ds(h * HROWS, HROWS)]
        send(here, here, a2_send.at[s, way, h], a2_got.at[s, way, h], z_dev(1 if way == 0 else 3))

    for s in (0, 1):
        for d in (1, 3, 2):
            got(first_recv.at[s, (first_pos[s] - d) % 4], f_send.at[s, d], f_got.at[s, d])
        pieces = []
        for j in range(4):
            piece = f32(first_recv[s, j])
            pieces.append(jnp.concatenate([piece[:ROWS], piece[ROWS:]], axis=1))
        w[s, last_pos[s] * 4 + z] = jnp.concatenate(pieces, axis=0).astype(BF16)
        send_second(s, 0, 0)
        send_second(s, 1, 1)
    for s in (0, 1):
        send_second(s, 0, 1)
        send_second(s, 1, 0)

    def add_rows(dst, rows, sources):
        def step(i, _):
            at = pl.ds(pl.multiple_of(i * 48, 48), 48)
            total = f32(sources[0][at])
            for ref in sources[1:]:
                total = total + f32(ref[at])
            dst[at] = total.astype(dst.dtype)
            return 0
        lax.fori_loop(0, rows // 48, step, 0)

    def hand_on(n):
        for s in (1, 0):
            for way, k in ((0, TO_RIGHT[n]), (1, TO_LEFT[n])):
                got(r1x.at[s, way, n], s1x_send.at[s, way, n], s1x_got.at[s, way, n])
                here = g.at[s, chunk_at(s, 1 if way == 0 else 3, k)]
                add_rows(here, CHUNK, [here, r1x.at[s, way, n]])
                send_one(s, way, k)

    def second_at(s, d, h):
        return w.at[s, last_pos[s] * 4 + (z + d) % 4, pl.ds(h * HROWS, HROWS)]

    def wait_second(s, way, h):
        got(second_at(s, 3 if way == 0 else 1, h), a2_send.at[s, way, h], a2_got.at[s, way, h])

    hand_on(0)
    for s in (0, 1):
        for way in (0, 1):
            wait_second(s, way, way)
            here = second_at(s, 3 if way == 0 else 1, way)
            send(here, here, a2x_send.at[s, way], a2x_got.at[s, way], z_dev(1 if way == 0 else 3))
    hand_on(1)

    def close(s, k, h, extra=()):
        rows = pl.ds(h * HROWS, HROWS)
        here = g.at[s, chunk_at(s, 0, k), rows]
        add_rows(here, HROWS, [here, r1.at[s, 0, k, rows], r1.at[s, 1, k, rows], *extra])
        return here

    def wait_last(k):
        for s in (0, 1):
            for way in (0, 1):
                got(r1.at[s, way, k], s1_send.at[s, way, k], s1_got.at[s, way, k])

    wait_last(2)
    for s in (0, 1):
        for way in (0, 1):
            send(close(s, 2, way), r2x.at[s, way], s2x_send.at[s, way], s2x_got.at[s, way],
                 z_dev(1 if way == 0 else 3))

    def send_third(s, way, k):
        here = w.at[s, chunk_at(s, 0, k)]
        send(here, here, a3_send.at[s, way, k], a3_got.at[s, way, k], last_dev[s](1 if way == 0 else 3))

    def hand_third(s, way, k):
        here = w.at[s, chunk_at(s, 3 if way == 0 else 1, k)]
        got(here, a3_send.at[s, way, k], a3_got.at[s, way, k])
        send(here, here, a3x_send.at[s, k], a3x_got.at[s, k], last_dev[s](1 if way == 0 else 3))

    for s in (0, 1):
        for way in (0, 1):
            send_third(s, way, 0)

    def send_plain_z(s, way):
        k, h = (1, 1) if way == 0 else (3, 0)
        send(close(s, k, h), r2.at[s, way, h], s2_send.at[s, way, h], s2_got.at[s, way, h],
             z_dev(1 if way == 0 else 3))

    wait_last(1)
    for s in (0, 1):
        send_plain_z(s, 0)
    wait_last(3)
    for s in (0, 1):
        send_plain_z(s, 1)

    for s in (0, 1):
        for way in (0, 1):
            wait_second(s, way, 1 - way)
    for k in (1, 3):
        for s in (0, 1):
            for way in (0, 1):
                send_third(s, way, k)
    for s in (0, 1):
        for way in (0, 1):
            got(second_at(s, 2, way), a2x_send.at[s, way], a2x_got.at[s, way])
    for s in (0, 1):
        for way in (0, 1):
            send_third(s, way, 2)

    for s in (0, 1):
        for way in (0, 1):
            got(r2x.at[s, way], s2x_send.at[s, way], s2x_got.at[s, way])
            k, h = (1, 0) if way == 0 else (3, 1)
            send(close(s, k, h, (r2x.at[s, way],)), r2.at[s, way, h],
                 s2_send.at[s, way, h], s2_got.at[s, way, h], z_dev(1 if way == 0 else 3))

    for n in (1, 0):
        for s in (0, 1):
            hand_third(s, 0, TO_RIGHT[n])
            hand_third(s, 1, TO_LEFT[1 - n])

    wait_last(0)
    for s in (0, 1):
        for h in (0, 1):
            for way in (0, 1):
                got(r2.at[s, way, h], s2_send.at[s, way, h], s2_got.at[s, way, h])
            rows = pl.ds(h * HROWS, HROWS)
            add_rows(third.at[s, rows], HROWS,
                     [g.at[s, chunk_at(s, 0, 0), rows], r1.at[s, 0, 0, rows], r1.at[s, 1, 0, rows],
                      r2.at[s, 0, h], r2.at[s, 1, h]])
        for d in (2, 1, 3):
            at = pl.multiple_of(((first_pos[s] + d) % 4) * ROWS, 8)
            send(third.at[s, pl.ds(at, ROWS)], r3.at[s, d], s3_send.at[s, d], s3_got.at[s, d], first_dev[s](d))

    for s in (0, 1):
        for way, ks in ((0, TO_LEFT), (1, TO_RIGHT)):
            for k in ks:
                got(w.at[s, chunk_at(s, 3 if way == 0 else 1, k)], a3_send.at[s, way, k], a3_got.at[s, way, k])
        for k in range(4):
            got(w.at[s, chunk_at(s, 2, k)], a3x_send.at[s, k], a3x_got.at[s, k])

    def unpack(k, _):
        for a in range(4):
            low = a * ROWS - 8 * (a % 2)
            pieces = []
            for b in range(4):
                piece = f32(w[0, b * 4 + k, low:low + ROWS + 8])
                skip = 8 * (a % 2)
                pieces.append(piece[skip:skip + ROWS])
            wnat[a * 4 + k] = jnp.concatenate(pieces, axis=0).astype(BF16)
        return 0
    lax.fori_loop(0, 4, unpack, 0)

    scale = D ** (-0.5)

    def nt(lhs, rhs):
        return lax.dot_general(lhs, rhs, (((1,), (1,)), ((), ())), preferred_element_type=F32)

    def weight(ref, b):
        return ref[pl.ds(b * 4, 4)].reshape(BLOCK, HALF)

    def back(b, _):
        at = pl.multiple_of(b * BLOCK, 128)
        part = nt(kgv[:, :HALF], weight(wnat, b)) + nt(kgv[:, HALF:], weight(w.at[1], b))
        igv[:, pl.ds(at, BLOCK)] = (part * scale).astype(BF16)
        return 0
    lax.fori_loop(0, 4, back, 0)
    store_ig = pltpu.make_async_copy(igv, ig_hbm, store_sem.at[0])
    store_ig.start()
    for s, ref in ((0, wnat), (1, w.at[1])):
        total = None
        for b in range(4):
            part = jnp.dot(xv[:, b * BLOCK:(b + 1) * BLOCK], weight(ref, b), preferred_element_type=F32)
            total = part if total is None else total + part
        keysv[:, s * HALF:(s + 1) * HALF] = (total * scale).astype(BF16)
    store_keys = pltpu.make_async_copy(keysv, keys_hbm, store_sem.at[1])
    store_keys.start()

    for s in (0, 1):
        at = pl.multiple_of(first_pos[s] * ROWS, 8)
        total = third[s, pl.ds(at, ROWS)]
        for d in (1, 3, 2):
            got(r3.at[s, d], s3_send.at[s, d], s3_got.at[s, d])
            total = total + r3[s, d]
        gradv[:, s * HALF:(s + 1) * HALF] = total * scale
    store_grad = pltpu.make_async_copy(gradv, grad_hbm, store_sem.at[2])
    store_grad.start()

    for copy in pending:
        copy.wait_send()
    store_ig.wait()
    store_keys.wait()
    store_grad.wait()


def exchange(normed, key_grad, local):
    any_space = pl.BlockSpec(memory_space=pl.ANY)
    dma = pltpu.SemaphoreType.DMA
    return pl.pallas_call(
        kernel,
        out_shape=(
            jax.ShapeDtypeStruct((TOK, KD), BF16),
            jax.ShapeDtypeStruct((TOK, D), BF16),
            jax.ShapeDtypeStruct((ROWS, KD), F32),
        ),
        in_specs=[any_space] * 3,
        out_specs=(any_space,) * 3,
        scratch_shapes=[
            pltpu.VMEM((TOK, D), BF16),
            pltpu.VMEM((TOK, KD), BF16),
            pltpu.VMEM((ROWS, KD), F32),
            pltpu.VMEM((TOK, KD), BF16),
            pltpu.VMEM((TOK, D), BF16),
            pltpu.VMEM((ROWS, KD), F32),
            pltpu.VMEM((2, 16, CHUNK, HALF), BF16),
            pltpu.VMEM((16, CHUNK, HALF), BF16),
            pltpu.VMEM((2, 16, CHUNK, HALF), BF16),
            pltpu.VMEM((D, HALF), F32),
            pltpu.VMEM((2, 2 * ROWS, HALF // 2), BF16),
            pltpu.VMEM((2, 4, 2 * ROWS, HALF // 2), BF16),
            pltpu.VMEM((2, 2, 4, CHUNK, HALF), BF16),
            pltpu.VMEM((2, 2, 2, CHUNK, HALF), BF16),
            pltpu.VMEM((2, 2, 2, HROWS, HALF), BF16),
            pltpu.VMEM((2, 2, HROWS, HALF), BF16),
            pltpu.VMEM((2, CHUNK, HALF), F32),
            pltpu.VMEM((2, 4, ROWS, HALF), F32),
            dma((3,)), dma((3,)),
            dma((2, 4)), dma((2, 4)),
            dma((2, 2, 2)), dma((2, 2, 2)), dma((2, 2)), dma((2, 2)),
            dma((2, 2, 4)), dma((2, 2, 4)), dma((2, 4)), dma((2, 4)),
            dma((2, 2, 2)), dma((2, 2, 2)), dma((2, 2, 4)), dma((2, 2, 4)),
            dma((2, 2)), dma((2, 2)), dma((2, 2, 2)), dma((2, 2, 2)), dma((2, 4)), dma((2, 4)),
        ],
        compiler_params=pltpu.CompilerParams(
            collective_id=0, has_side_effects=True, vmem_limit_bytes=60 * 2**20
        ),
        cost_estimate=pl.CostEstimate(
            flops=6 * TOK * D * KD, bytes_accessed=10 * 2**20, transcendentals=0
        ),
        name="exchange",
    )(normed, key_grad, local)


def nesterov(outer_grad, anchor_rows, moment_rows):
    moment_new = outer_mu * moment_rows + outer_grad
    anchor_new = anchor_rows - outer_rate * (outer_grad + outer_mu * moment_new)
    return (anchor_new, moment_new)


def body(normed, key_grad, master, first_moment, second_moment, anchor, momentum, inner_step):
    local, first_old, second_old = master[0], first_moment[0], second_moment[0]
    summed = lax.psum(anchor - local, "rep")
    keys, input_grad, gradient = exchange(normed, key_grad, local)
    anchor_new, moment_new = nesterov(summed / lax.axis_size("rep"), anchor, momentum)
    count_float = inner_step[0].astype(F32)
    fix_first = 1.0 - jnp.power(F32(beta_first), count_float)
    fix_second = 1.0 - jnp.power(F32(beta_second), count_float)
    first_new = beta_first * first_old + (1.0 - beta_first) * gradient
    second_new = beta_second * second_old + (1.0 - beta_second) * gradient * gradient
    direction = first_new / fix_first / (jnp.sqrt(second_new / fix_second) + epsilon)
    stepped = local - inner_rate * (direction + weight_decay * local)
    merged = mix_weight * stepped + (1.0 - mix_weight) * anchor_new
    return (
        keys,
        input_grad,
        merged[None],
        first_new[None],
        second_new[None],
        anchor_new,
        moment_new,
    )


def solution(mesh):
    in_specs = (
        P(("rep", "fsdp"), None),
        P(("rep", "fsdp"), None),
        P("rep", "fsdp", None),
        P("rep", "fsdp", None),
        P("rep", "fsdp", None),
        P("fsdp", None),
        P("fsdp", None),
        P(),
    )
    out_specs = (
        P(("rep", "fsdp"), None),
        P(("rep", "fsdp"), None),
        P("rep", "fsdp", None),
        P("rep", "fsdp", None),
        P("rep", "fsdp", None),
        P("fsdp", None),
        P("fsdp", None),
    )
    return jax.shard_map(body, mesh=mesh, in_specs=in_specs, out_specs=out_specs, check_vma=False)
```

```python
import math

import jax
import jax.numpy as jnp
from jax import lax
from jax.experimental import pallas as pl
from jax.experimental.pallas import tpu as pltpu
from jax.sharding import PartitionSpec as P

beta_first = 0.9
beta_second = 0.95
inner_rate = 0.1
weight_decay = 0.1
epsilon = 1e-08
outer_rate = 0.7
outer_mu = 0.9
mix_weight = 0.5

MESH = pl.DeviceIdType.MESH
D, KD, TOK = 4608, 1024, 384
ROWS = 72
HALF = KD // 2
CHUNK = 4 * ROWS
HROWS = CHUNK // 2
BLOCK = 4 * CHUNK
TO_RIGHT = (2, 0)
TO_LEFT = (1, 3)
F32, BF16 = jnp.float32, jnp.bfloat16


def f32(v):
    return v.astype(F32)


def kernel(
    step_ref, normed_hbm, kg_hbm, master_hbm, moment1_hbm, moment2_hbm, anchor_hbm, momentum_hbm,
    keysv, igv, merged_ref, first_ref, second_ref, anchor_ref, momentum_ref,
    xv, kgv, mv, m1v, m2v, av, ov, delta, core_got, half_sum, z_got, half_got,
    w, g, gnat, first_send, first_recv,
    r1, r1x, r2, r2x, third, r3,
    load_sem, o_send, o_got,
    f_send, f_got, a2_send, a2_got, a2x_send, a2x_got,
    a3_send, a3_got, a3x_send, a3x_got,
    s1x_send, s1x_got, s1_send, s1_got,
    s2x_send, s2x_got, s2_send, s2_got, s3_send, s3_got,
):
    rep = lax.axis_index("rep")
    shard = lax.axis_index("fsdp")
    x, z, y = shard // 16, (shard // 4) % 4, shard % 4

    def dev(dx, dz, dy):
        return (rep, ((x + dx) % 4) * 16 + ((z + dz) % 4) * 4 + (y + dy) % 4)

    first_pos, last_pos = (x, y), (y, x)
    first_dev = (lambda d: dev(d, 0, 0), lambda d: dev(0, 0, d))
    last_dev = (first_dev[1], first_dev[0])

    def z_dev(d):
        return dev(0, d, 0)

    core = rep % 2
    core_dev = (rep + 1 - 2 * core, shard)
    pair_dev = ((rep + 2) % 4, shard)

    pending = []

    def send(src, dst, ssem, rsem, target):
        copy = pltpu.make_async_remote_copy(
            src_ref=src, dst_ref=dst, send_sem=ssem, recv_sem=rsem,
            device_id=target, device_id_type=MESH,
        )
        copy.start()
        pending.append(copy)

    def got(dst, ssem, rsem):
        pltpu.make_async_remote_copy(
            src_ref=dst, dst_ref=dst, send_sem=ssem, recv_sem=rsem,
            device_id=z_dev(1), device_id_type=MESH,
        ).wait_recv()

    loads = [
        pltpu.make_async_copy(master_hbm, mv, load_sem.at[0]),
        pltpu.make_async_copy(normed_hbm, xv, load_sem.at[1]),
        pltpu.make_async_copy(kg_hbm, kgv, load_sem.at[2]),
        pltpu.make_async_copy(anchor_hbm, av, load_sem.at[3]),
        pltpu.make_async_copy(moment1_hbm, m1v, load_sem.at[4]),
        pltpu.make_async_copy(moment2_hbm, m2v, load_sem.at[5]),
        pltpu.make_async_copy(momentum_hbm, ov, load_sem.at[6]),
    ]
    for copy in loads:
        copy.start()

    barrier = pltpu.get_barrier_semaphore()
    peers = [first_dev[s](d) for s in (0, 1) for d in (1, 3, 2)] + [z_dev(1), z_dev(3), core_dev, pair_dev]
    for peer in peers:
        pl.semaphore_signal(barrier, inc=1, device_id=peer, device_id_type=MESH)
    pl.semaphore_wait(barrier, len(peers))

    loads[0].wait()
    for s in (0, 1):
        own = mv[:, s * HALF:(s + 1) * HALF]
        packed = jnp.concatenate([own[:, :HALF // 2], own[:, HALF // 2:]], axis=0).astype(BF16)
        first_send[s] = packed
        first_recv[s, first_pos[s]] = packed
        for d in (1, 3, 2):
            send(first_send.at[s], first_recv.at[s, first_pos[s]],
                 f_send.at[s, d], f_got.at[s, d], first_dev[s](d))

    loads[3].wait()
    delta[...] = av[...] - mv[...]
    send(delta, core_got, o_send.at[0], o_got.at[0], core_dev)

    def chunk_at(s, d, k):
        return ((last_pos[s] + d) % 4) * 4 + (z + k) % 4

    def send_relay(s):
        for n, k in enumerate(TO_RIGHT):
            send(g.at[s, chunk_at(s, 2, k)], r1x.at[s, 0, n],
                 s1x_send.at[s, 0, n], s1x_got.at[s, 0, n], last_dev[s](1))
        for n, k in enumerate(TO_LEFT):
            send(g.at[s, chunk_at(s, 2, k)], r1x.at[s, 1, n],
                 s1x_send.at[s, 1, n], s1x_got.at[s, 1, n], last_dev[s](3))

    def send_one(s, way, k):
        send(g.at[s, chunk_at(s, 1 if way == 0 else 3, k)], r1.at[s, way, k],
             s1_send.at[s, way, k], s1_got.at[s, way, k], last_dev[s](1 if way == 0 else 3))

    loads[1].wait()
    loads[2].wait()

    def tn(lhs, rhs):
        return lax.dot_general(lhs, rhs, (((0,), (0,)), ((), ())), preferred_element_type=F32)

    def grad_one(block):
        def step(i, _):
            at = pl.multiple_of(block * BLOCK + i * TOK, 128)
            part = tn(xv[:, pl.ds(at, TOK)], kgv[:, HALF:]).astype(BF16)
            flat = g.at[1, pl.ds(block * 4, 4)]
            for n in range(TOK // 96):
                row = i * TOK + n * 96
                flat[row // CHUNK, pl.ds(pl.multiple_of(row % CHUNK, 96), 96)] = part[n * 96:(n + 1) * 96]
            return 0
        lax.fori_loop(0, BLOCK // TOK, step, 0)

    grad_one((x + 2) % 4)
    send_relay(1)

    got(core_got, o_send.at[0], o_got.at[0])
    mine = pl.ds(pl.multiple_of(core * HALF, 128), HALF)
    half_sum[...] = delta[:, mine] + core_got[:, mine]
    send(half_sum, z_got, o_send.at[1], o_got.at[1], pair_dev)

    def grad_zero(i, _):
        at = pl.multiple_of(i * TOK, 128)
        gnat[pl.ds(at, TOK)] = tn(xv[:, pl.ds(at, TOK)], kgv[:, :HALF])
        return 0
    lax.fori_loop(0, D // TOK, grad_zero, 0)

    def pack(block):
        def step(k, _):
            for half in (0, 1):
                pieces = [
                    gnat[pl.ds(pl.multiple_of(a * BLOCK + k * CHUNK + block * ROWS, 8), ROWS)]
                    for a in (2 * half, 2 * half + 1)
                ]
                g[0, block * 4 + k, half * HROWS:(half + 1) * HROWS] = jnp.concatenate(pieces, axis=0).astype(BF16)
            return 0
        lax.fori_loop(0, 4, step, 0)

    pack((y + 2) % 4)
    send_relay(0)
    for d in (1, 3):
        grad_one((x + d) % 4)
        pack((y + d) % 4)
        for s in (1, 0):
            way = 0 if d == 1 else 1
            for k in (TO_LEFT if d == 1 else TO_RIGHT):
                send_one(s, way, k)
    grad_one(x)
    pack(y)

    def send_second(s, way, h):
        here = w.at[s, last_pos[s] * 4 + z, pl.ds(h * HROWS, HROWS)]
        send(here, here, a2_send.at[s, way, h], a2_got.at[s, way, h], z_dev(1 if way == 0 else 3))

    for s in (0, 1):
        for d in (1, 3, 2):
            got(first_recv.at[s, (first_pos[s] - d) % 4], f_send.at[s, d], f_got.at[s, d])
        pieces = []
        for j in range(4):
            piece = f32(first_recv[s, j])
            pieces.append(jnp.concatenate([piece[:ROWS], piece[ROWS:]], axis=1))
        w[s, last_pos[s] * 4 + z] = jnp.concatenate(pieces, axis=0).astype(BF16)
        send_second(s, 0, 0)
        send_second(s, 1, 1)
    for s in (0, 1):
        send_second(s, 0, 1)
        send_second(s, 1, 0)

    def add_rows(dst, rows, sources):
        def step(i, _):
            at = pl.ds(pl.multiple_of(i * 48, 48), 48)
            total = f32(sources[0][at])
            for ref in sources[1:]:
                total = total + f32(ref[at])
            dst[at] = total.astype(dst.dtype)
            return 0
        lax.fori_loop(0, rows // 48, step, 0)

    def hand_on(n):
        for s in (1, 0):
            for way, k in ((0, TO_RIGHT[n]), (1, TO_LEFT[n])):
                got(r1x.at[s, way, n], s1x_send.at[s, way, n], s1x_got.at[s, way, n])
                here = g.at[s, chunk_at(s, 1 if way == 0 else 3, k)]
                add_rows(here, CHUNK, [here, r1x.at[s, way, n]])
                send_one(s, way, k)

    def second_at(s, d, h):
        return w.at[s, last_pos[s] * 4 + (z + d) % 4, pl.ds(h * HROWS, HROWS)]

    def wait_second(s, way, h):
        got(second_at(s, 3 if way == 0 else 1, h), a2_send.at[s, way, h], a2_got.at[s, way, h])

    got(z_got, o_send.at[1], o_got.at[1])
    z_got[...] = half_sum[...] + z_got[...]
    send(z_got, half_got.at[:, mine], o_send.at[2], o_got.at[2], core_dev)

    hand_on(0)
    for s in (0, 1):
        for way in (0, 1):
            wait_second(s, way, way)
            here = second_at(s, 3 if way == 0 else 1, way)
            send(here, here, a2x_send.at[s, way], a2x_got.at[s, way], z_dev(1 if way == 0 else 3))
    hand_on(1)

    def close(s, k, h, extra=()):
        rows = pl.ds(h * HROWS, HROWS)
        here = g.at[s, chunk_at(s, 0, k), rows]
        add_rows(here, HROWS, [here, r1.at[s, 0, k, rows], r1.at[s, 1, k, rows], *extra])
        return here

    def wait_last(k):
        for s in (0, 1):
            for way in (0, 1):
                got(r1.at[s, way, k], s1_send.at[s, way, k], s1_got.at[s, way, k])

    wait_last(2)
    for s in (0, 1):
        for way in (0, 1):
            send(close(s, 2, way), r2x.at[s, way], s2x_send.at[s, way], s2x_got.at[s, way],
                 z_dev(1 if way == 0 else 3))

    def send_third(s, way, k):
        here = w.at[s, chunk_at(s, 0, k)]
        send(here, here, a3_send.at[s, way, k], a3_got.at[s, way, k], last_dev[s](1 if way == 0 else 3))

    def hand_third(s, way, k):
        here = w.at[s, chunk_at(s, 3 if way == 0 else 1, k)]
        got(here, a3_send.at[s, way, k], a3_got.at[s, way, k])
        send(here, here, a3x_send.at[s, k], a3x_got.at[s, k], last_dev[s](1 if way == 0 else 3))

    for s in (0, 1):
        for way in (0, 1):
            send_third(s, way, 0)

    def send_plain_z(s, way):
        k, h = (1, 1) if way == 0 else (3, 0)
        send(close(s, k, h), r2.at[s, way, h], s2_send.at[s, way, h], s2_got.at[s, way, h],
             z_dev(1 if way == 0 else 3))

    wait_last(1)
    for s in (0, 1):
        send_plain_z(s, 0)
    wait_last(3)
    for s in (0, 1):
        send_plain_z(s, 1)

    for s in (0, 1):
        for way in (0, 1):
            wait_second(s, way, 1 - way)
    for k in (1, 3):
        for s in (0, 1):
            for way in (0, 1):
                send_third(s, way, k)
    for s in (0, 1):
        for way in (0, 1):
            got(second_at(s, 2, way), a2x_send.at[s, way], a2x_got.at[s, way])
    for s in (0, 1):
        for way in (0, 1):
            send_third(s, way, 2)

    for s in (0, 1):
        for way in (0, 1):
            got(r2x.at[s, way], s2x_send.at[s, way], s2x_got.at[s, way])
            k, h = (1, 0) if way == 0 else (3, 1)
            send(close(s, k, h, (r2x.at[s, way],)), r2.at[s, way, h],
                 s2_send.at[s, way, h], s2_got.at[s, way, h], z_dev(1 if way == 0 else 3))

    for n in (1, 0):
        for s in (0, 1):
            hand_third(s, 0, TO_RIGHT[n])
            hand_third(s, 1, TO_LEFT[1 - n])

    wait_last(0)
    for s in (0, 1):
        for h in (0, 1):
            for way in (0, 1):
                got(r2.at[s, way, h], s2_send.at[s, way, h], s2_got.at[s, way, h])
            rows = pl.ds(h * HROWS, HROWS)
            add_rows(third.at[s, rows], HROWS,
                     [g.at[s, chunk_at(s, 0, 0), rows], r1.at[s, 0, 0, rows], r1.at[s, 1, 0, rows],
                      r2.at[s, 0, h], r2.at[s, 1, h]])
        for d in (2, 1, 3):
            at = pl.multiple_of(((first_pos[s] + d) % 4) * ROWS, 8)
            send(third.at[s, pl.ds(at, ROWS)], r3.at[s, d], s3_send.at[s, d], s3_got.at[s, d], first_dev[s](d))

    for s in (0, 1):
        for way, ks in ((0, TO_LEFT), (1, TO_RIGHT)):
            for k in ks:
                got(w.at[s, chunk_at(s, 3 if way == 0 else 1, k)], a3_send.at[s, way, k], a3_got.at[s, way, k])
        for k in range(4):
            got(w.at[s, chunk_at(s, 2, k)], a3x_send.at[s, k], a3x_got.at[s, k])

    for copy in pending:
        copy.wait_send()
    pending.clear()
    wnat = g.at[0]

    def unpack(k, _):
        for a in range(4):
            low = a * ROWS - 8 * (a % 2)
            pieces = []
            for b in range(4):
                piece = f32(w[0, b * 4 + k, low:low + ROWS + 8])
                skip = 8 * (a % 2)
                pieces.append(piece[skip:skip + ROWS])
            wnat[a * 4 + k] = jnp.concatenate(pieces, axis=0).astype(BF16)
        return 0
    lax.fori_loop(0, 4, unpack, 0)

    scale = D ** (-0.5)

    def nt(lhs, rhs):
        return lax.dot_general(lhs, rhs, (((1,), (1,)), ((), ())), preferred_element_type=F32)

    def weight(ref, b):
        return ref[pl.ds(b * 4, 4)].reshape(BLOCK, HALF)

    def back(b, _):
        at = pl.multiple_of(b * BLOCK, 128)
        part = nt(kgv[:, :HALF], weight(wnat, b)) + nt(kgv[:, HALF:], weight(w.at[1], b))
        igv[:, pl.ds(at, BLOCK)] = (part * scale).astype(BF16)
        return 0
    lax.fori_loop(0, 4, back, 0)
    for s, ref in ((0, wnat), (1, w.at[1])):
        total = None
        for b in range(4):
            part = jnp.dot(xv[:, b * BLOCK:(b + 1) * BLOCK], weight(ref, b), preferred_element_type=F32)
            total = part if total is None else total + part
        keysv[:, s * HALF:(s + 1) * HALF] = (total * scale).astype(BF16)

    for copy in loads[4:]:
        copy.wait()
    other = pl.ds(pl.multiple_of((1 - core) * HALF, 128), HALF)
    got(half_got.at[:, other], o_send.at[2], o_got.at[2])
    half_got[:, mine] = z_got[...]
    outer_grad = half_got[...] * (1.0 / lax.axis_size("rep"))
    momentum_new = outer_mu * ov[...] + outer_grad
    anchor_new = av[...] - outer_rate * (outer_grad + outer_mu * momentum_new)
    momentum_ref[...] = momentum_new
    anchor_ref[...] = anchor_new

    count = jnp.full((1, HALF), step_ref[0].astype(F32), F32)
    fix_first = 1.0 / (1.0 - jnp.exp(count * math.log(beta_first)))
    fix_second = 1.0 / (1.0 - jnp.exp(count * math.log(beta_second)))
    for s in (0, 1):
        at = pl.multiple_of(first_pos[s] * ROWS, 8)
        total = third[s, pl.ds(at, ROWS)]
        for d in (1, 3, 2):
            got(r3.at[s, d], s3_send.at[s, d], s3_got.at[s, d])
            total = total + r3[s, d]
        gradient = total * scale
        cols = slice(s * HALF, (s + 1) * HALF)
        first_new = beta_first * m1v[:, cols] + (1.0 - beta_first) * gradient
        second_new = beta_second * m2v[:, cols] + (1.0 - beta_second) * gradient * gradient
        direction = first_new * fix_first / (jnp.sqrt(second_new * fix_second) + epsilon)
        local = mv[:, cols]
        stepped = local - inner_rate * (direction + weight_decay * local)
        first_ref[:, cols] = first_new
        second_ref[:, cols] = second_new
        merged_ref[:, cols] = mix_weight * stepped + (1.0 - mix_weight) * anchor_ref[:, cols]

    for copy in pending:
        copy.wait_send()


def exchange(inner_step, *arrays):
    dma = pltpu.SemaphoreType.DMA
    rows = (ROWS, KD)
    return pl.pallas_call(
        kernel,
        out_shape=(
            pltpu.VMEM((TOK, KD), BF16),
            pltpu.VMEM((TOK, D), BF16),
        ) + (pltpu.VMEM(rows, F32),) * 5,
        in_specs=[pl.BlockSpec(memory_space=pltpu.SMEM)] + [pl.BlockSpec(memory_space=pl.ANY)] * 7,
        out_specs=(pl.BlockSpec(memory_space=pltpu.VMEM),) * 7,
        scratch_shapes=[
            pltpu.VMEM((TOK, D), BF16),
            pltpu.VMEM((TOK, KD), BF16),
            pltpu.VMEM(rows, F32),
            pltpu.VMEM(rows, F32),
            pltpu.VMEM(rows, F32),
            pltpu.VMEM(rows, F32),
            pltpu.VMEM(rows, F32),
            pltpu.VMEM(rows, F32),
            pltpu.VMEM(rows, F32),
            pltpu.VMEM((ROWS, HALF), F32),
            pltpu.VMEM((ROWS, HALF), F32),
            pltpu.VMEM(rows, F32),
            pltpu.VMEM((2, 16, CHUNK, HALF), BF16),
            pltpu.VMEM((2, 16, CHUNK, HALF), BF16),
            pltpu.VMEM((D, HALF), F32),
            pltpu.VMEM((2, 2 * ROWS, HALF // 2), BF16),
            pltpu.VMEM((2, 4, 2 * ROWS, HALF // 2), BF16),
            pltpu.VMEM((2, 2, 4, CHUNK, HALF), BF16),
            pltpu.VMEM((2, 2, 2, CHUNK, HALF), BF16),
            pltpu.VMEM((2, 2, 2, HROWS, HALF), BF16),
            pltpu.VMEM((2, 2, HROWS, HALF), BF16),
            pltpu.VMEM((2, CHUNK, HALF), F32),
            pltpu.VMEM((2, 4, ROWS, HALF), F32),
            dma((7,)), dma((3,)), dma((3,)),
            dma((2, 4)), dma((2, 4)),
            dma((2, 2, 2)), dma((2, 2, 2)), dma((2, 2)), dma((2, 2)),
            dma((2, 2, 4)), dma((2, 2, 4)), dma((2, 4)), dma((2, 4)),
            dma((2, 2, 2)), dma((2, 2, 2)), dma((2, 2, 4)), dma((2, 2, 4)),
            dma((2, 2)), dma((2, 2)), dma((2, 2, 2)), dma((2, 2, 2)), dma((2, 4)), dma((2, 4)),
        ],
        compiler_params=pltpu.CompilerParams(
            collective_id=0, has_side_effects=True, vmem_limit_bytes=48 * 2**20
        ),
        cost_estimate=pl.CostEstimate(
            flops=6 * TOK * D * KD, bytes_accessed=10 * 2**20, transcendentals=0
        ),
        name="exchange",
    )(inner_step, *arrays)


def store_kernel(*refs):
    n = len(refs) // 2
    copies = [pltpu.make_async_copy(refs[i], refs[n + i], refs[-1].at[i]) for i in range(n)]
    for copy in copies:
        copy.start()
    for copy in copies:
        copy.wait()


def store(arrays):
    any_space = pl.BlockSpec(memory_space=pl.ANY)
    return pl.pallas_call(
        store_kernel,
        out_shape=tuple(jax.ShapeDtypeStruct(a.shape, a.dtype) for a in arrays),
        in_specs=[pl.BlockSpec(memory_space=pltpu.VMEM)] * len(arrays),
        out_specs=(any_space,) * len(arrays),
        scratch_shapes=[pltpu.SemaphoreType.DMA((len(arrays),))],
        compiler_params=pltpu.CompilerParams(vmem_limit_bytes=2**20),
        name="store",
    )(*[pltpu.with_memory_space_constraint(a, pltpu.VMEM) for a in arrays])


def body(normed, key_grad, master, first_moment, second_moment, anchor, momentum, inner_step):
    results = exchange(
        inner_step, normed, key_grad, master[0], first_moment[0], second_moment[0], anchor, momentum
    )
    keys, input_grad, merged, first_new, second_new, anchor_new, momentum_new = store(results)
    return (
        keys,
        input_grad,
        merged[None],
        first_new[None],
        second_new[None],
        anchor_new,
        momentum_new,
    )


def solution(mesh):
    in_specs = (
        P(("rep", "fsdp"), None),
        P(("rep", "fsdp"), None),
        P("rep", "fsdp", None),
        P("rep", "fsdp", None),
        P("rep", "fsdp", None),
        P("fsdp", None),
        P("fsdp", None),
        P(),
    )
    out_specs = (
        P(("rep", "fsdp"), None),
        P(("rep", "fsdp"), None),
        P("rep", "fsdp", None),
        P("rep", "fsdp", None),
        P("rep", "fsdp", None),
        P("fsdp", None),
        P("fsdp", None),
    )
    return jax.shard_map(body, mesh=mesh, in_specs=in_specs, out_specs=out_specs, check_vma=False)
```

```python
import math

import jax
import jax.numpy as jnp
from jax import lax
from jax.experimental import pallas as pl
from jax.experimental.pallas import tpu as pltpu
from jax.sharding import PartitionSpec as P

beta_first = 0.9
beta_second = 0.95
inner_rate = 0.1
weight_decay = 0.1
epsilon = 1e-08
outer_rate = 0.7
outer_mu = 0.9
mix_weight = 0.5

MESH = pl.DeviceIdType.MESH
D, KD, TOK = 4608, 1024, 384
ROWS = 72
HALF = KD // 2
CHUNK = 4 * ROWS
HROWS = CHUNK // 2
BLOCK = 4 * CHUNK
TO_RIGHT = (2, 0)
TO_LEFT = (1, 3)
F32, BF16 = jnp.float32, jnp.bfloat16


def f32(v):
    return v.astype(F32)


def kernel(
    step_hbm, normed_hbm, kg_hbm, master_hbm, moment1_hbm, moment2_hbm, anchor_hbm, momentum_hbm,
    keysv, igv, merged_ref, first_ref, second_ref, anchor_ref, momentum_ref,
    xv, kgv, mv, m1v, m2v, av, ov, delta, core_got, half_sum, z_got, half_got,
    w, g, gnat, keys_sum, packed, r1, r1x, r2, r2x, third, r3_send, r3, step_ref,
    load_sem, o_send, o_got,
    f_send, f_got, a2_send, a2_got, a2x_send, a2x_got,
    a3_send, a3_got, a3x_send, a3x_got,
    s1x_send, s1x_got, s1_send, s1_got,
    s2x_send, s2x_got, s2_send, s2_got, s3_send, s3_got,
):
    rep = lax.axis_index("rep")
    shard = lax.axis_index("fsdp")
    x, z, y = shard // 16, (shard // 4) % 4, shard % 4

    def dev(dx, dz, dy):
        return (rep, ((x + dx) % 4) * 16 + ((z + dz) % 4) * 4 + (y + dy) % 4)

    first_pos, last_pos = (x, y), (y, x)
    first_dev = (lambda d: dev(d, 0, 0), lambda d: dev(0, 0, d))
    last_dev = (first_dev[1], first_dev[0])

    def z_dev(d):
        return dev(0, d, 0)

    core = rep % 2
    core_dev = (rep + 1 - 2 * core, shard)
    pair_dev = ((rep + 2) % 4, shard)

    pending = []
    pending_sums = []

    def send(src, dst, ssem, rsem, target, queue=pending):
        copy = pltpu.make_async_remote_copy(
            src_ref=src, dst_ref=dst, send_sem=ssem, recv_sem=rsem,
            device_id=target, device_id_type=MESH,
        )
        copy.start()
        queue.append(copy)

    def got(dst, ssem, rsem):
        pltpu.make_async_remote_copy(
            src_ref=dst, dst_ref=dst, send_sem=ssem, recv_sem=rsem,
            device_id=z_dev(1), device_id_type=MESH,
        ).wait_recv()

    loads = [
        pltpu.make_async_copy(master_hbm, mv, load_sem.at[0]),
        pltpu.make_async_copy(normed_hbm, xv, load_sem.at[1]),
        pltpu.make_async_copy(kg_hbm, kgv, load_sem.at[2]),
        pltpu.make_async_copy(anchor_hbm, av, load_sem.at[3]),
        pltpu.make_async_copy(moment1_hbm, m1v, load_sem.at[4]),
        pltpu.make_async_copy(moment2_hbm, m2v, load_sem.at[5]),
        pltpu.make_async_copy(momentum_hbm, ov, load_sem.at[6]),
        pltpu.make_async_copy(step_hbm, step_ref, load_sem.at[7]),
    ]
    for copy in loads:
        copy.start()

    barrier = pltpu.get_barrier_semaphore()
    peers = [first_dev[s](d) for s in (0, 1) for d in (1, 3, 2)] + [z_dev(1), z_dev(3), core_dev, pair_dev]
    for peer in peers:
        pl.semaphore_signal(barrier, inc=1, device_id=peer, device_id_type=MESH)
    pl.semaphore_wait(barrier, len(peers))

    def pack_rows(v):
        return jnp.concatenate([v[:, :HALF // 2], v[:, HALF // 2:]], axis=0).astype(BF16)

    def unpack_rows(v):
        v = f32(v)
        return jnp.concatenate([v[:ROWS], v[ROWS:]], axis=1)

    def piece_at(s, dz, d):
        return packed.at[s, (z + dz) % 4, (first_pos[s] - d) % 4]

    def send_second(s, d):
        here = piece_at(s, 0, d)
        for way, dz in ((0, 1), (1, 3)):
            send(here, here, a2_send.at[s, way, d], a2_got.at[s, way, d], z_dev(dz))

    def wait_second(s, way, d):
        got(piece_at(s, 3 if way == 0 else 1, d), a2_send.at[s, way, d], a2_got.at[s, way, d])

    def hand_second(s, d):
        way = 0 if d in (0, 2) else 1
        wait_second(s, way, d)
        here = piece_at(s, 3 if way == 0 else 1, d)
        send(here, here, a2x_send.at[s, d], a2x_got.at[s, d], z_dev(1 if way == 0 else 3))

    loads[0].wait()
    for s in (0, 1):
        here = piece_at(s, 0, 0)
        here[...] = pack_rows(mv[:, s * HALF:(s + 1) * HALF])
        for d in (1, 3, 2):
            send(here, here, f_send.at[s, d], f_got.at[s, d], first_dev[s](d))
        send_second(s, 0)

    loads[3].wait()
    delta[...] = av[...] - mv[...]
    send(delta, core_got, o_send.at[0], o_got.at[0], core_dev)

    def chunk_at(s, d, k):
        return ((last_pos[s] + d) % 4) * 4 + (z + k) % 4

    def send_relay(s):
        for n, k in enumerate(TO_RIGHT):
            send(g.at[s, chunk_at(s, 2, k)], r1x.at[s, 0, n],
                 s1x_send.at[s, 0, n], s1x_got.at[s, 0, n], last_dev[s](1), pending_sums)
        for n, k in enumerate(TO_LEFT):
            send(g.at[s, chunk_at(s, 2, k)], r1x.at[s, 1, n],
                 s1x_send.at[s, 1, n], s1x_got.at[s, 1, n], last_dev[s](3), pending_sums)

    def send_one(s, way, k):
        send(g.at[s, chunk_at(s, 1 if way == 0 else 3, k)], r1.at[s, way, k],
             s1_send.at[s, way, k], s1_got.at[s, way, k], last_dev[s](1 if way == 0 else 3), pending_sums)

    loads[1].wait()
    loads[2].wait()

    def tn(lhs, rhs):
        return lax.dot_general(lhs, rhs, (((0,), (0,)), ((), ())), preferred_element_type=F32)

    def grad_block(block):
        def step(i, _):
            at = pl.multiple_of(block * BLOCK + i * TOK, 128)
            part = tn(xv[:, pl.ds(at, TOK)], kgv[...])
            gnat[pl.ds(at, TOK)] = part[:, :HALF]
            flat = g.at[1, pl.ds(block * 4, 4)]
            for n in range(TOK // 96):
                row = i * TOK + n * 96
                rows = pl.ds(pl.multiple_of(row % CHUNK, 96), 96)
                flat[row // CHUNK, rows] = part[n * 96:(n + 1) * 96, HALF:].astype(BF16)
            return 0
        lax.fori_loop(0, BLOCK // TOK, step, 0)

    def pack(block):
        def step(k, _):
            for half in (0, 1):
                pieces = [
                    gnat[pl.ds(pl.multiple_of(a * BLOCK + k * CHUNK + block * ROWS, 8), ROWS)]
                    for a in (2 * half, 2 * half + 1)
                ]
                g[0, block * 4 + k, half * HROWS:(half + 1) * HROWS] = jnp.concatenate(pieces, axis=0).astype(BF16)
            return 0
        lax.fori_loop(0, 4, step, 0)

    grad_block((x + 2) % 4)
    send_relay(1)

    got(core_got, o_send.at[0], o_got.at[0])
    mine = pl.ds(pl.multiple_of(core * HALF, 128), HALF)
    half_sum[...] = delta[:, mine] + core_got[:, mine]
    send(half_sum, z_got, o_send.at[1], o_got.at[1], pair_dev)

    for d in (1, 3):
        grad_block((x + d) % 4)
        for k in (TO_LEFT if d == 1 else TO_RIGHT):
            send_one(1, 0 if d == 1 else 1, k)
    grad_block(x)
    pack((y + 2) % 4)
    send_relay(0)

    for d in (1, 3, 2):
        for s in (0, 1):
            got(piece_at(s, 0, d), f_send.at[s, d], f_got.at[s, d])
            send_second(s, d)

    for d in (1, 3):
        pack((y + d) % 4)
        for k in (TO_LEFT if d == 1 else TO_RIGHT):
            send_one(0, 0 if d == 1 else 1, k)
    pack(y)

    def assemble(s, k):
        pieces = [unpack_rows(packed[s, (z + k) % 4, j]) for j in range(4)]
        w[s, chunk_at(s, 0, k)] = jnp.concatenate(pieces, axis=0).astype(BF16)

    def add_rows(dst, rows, sources):
        def step(i, _):
            at = pl.ds(pl.multiple_of(i * 48, 48), 48)
            total = f32(sources[0][at])
            for ref in sources[1:]:
                total = total + f32(ref[at])
            dst[at] = total.astype(dst.dtype)
            return 0
        lax.fori_loop(0, rows // 48, step, 0)

    def hand_on(n):
        for s in (1, 0):
            for way, k in ((0, TO_RIGHT[n]), (1, TO_LEFT[n])):
                got(r1x.at[s, way, n], s1x_send.at[s, way, n], s1x_got.at[s, way, n])
                here = g.at[s, chunk_at(s, 1 if way == 0 else 3, k)]
                add_rows(here, CHUNK, [here, r1x.at[s, way, n]])
                send_one(s, way, k)

    got(z_got, o_send.at[1], o_got.at[1])
    z_got[...] = half_sum[...] + z_got[...]
    send(z_got, half_got.at[:, mine], o_send.at[2], o_got.at[2], core_dev)

    hand_on(0)
    for d in (0, 1, 3):
        for s in (0, 1):
            hand_second(s, d)
    hand_on(1)
    for s in (0, 1):
        hand_second(s, 2)

    def close(s, k, h, extra=()):
        rows = pl.ds(h * HROWS, HROWS)
        here = g.at[s, chunk_at(s, 0, k), rows]
        add_rows(here, HROWS, [here, r1.at[s, 0, k, rows], r1.at[s, 1, k, rows], *extra])
        return here

    def wait_last(k):
        for s in (0, 1):
            for way in (0, 1):
                got(r1.at[s, way, k], s1_send.at[s, way, k], s1_got.at[s, way, k])

    wait_last(2)
    for s in (0, 1):
        for way in (0, 1):
            send(close(s, 2, way), r2x.at[s, way], s2x_send.at[s, way], s2x_got.at[s, way],
                 z_dev(1 if way == 0 else 3), pending_sums)

    def send_third(s, way, k):
        here = w.at[s, chunk_at(s, 0, k)]
        send(here, here, a3_send.at[s, way, k], a3_got.at[s, way, k], last_dev[s](1 if way == 0 else 3))

    def hand_third(s, way, k):
        here = w.at[s, chunk_at(s, 3 if way == 0 else 1, k)]
        got(here, a3_send.at[s, way, k], a3_got.at[s, way, k])
        send(here, here, a3x_send.at[s, k], a3x_got.at[s, k], last_dev[s](1 if way == 0 else 3))

    for s in (0, 1):
        assemble(s, 0)
        for way in (0, 1):
            send_third(s, way, 0)

    def send_plain_z(s, way):
        k, h = (1, 1) if way == 0 else (3, 0)
        send(close(s, k, h), r2.at[s, way, h], s2_send.at[s, way, h], s2_got.at[s, way, h],
             z_dev(1 if way == 0 else 3), pending_sums)

    wait_last(1)
    for s in (0, 1):
        send_plain_z(s, 0)
    wait_last(3)
    for s in (0, 1):
        send_plain_z(s, 1)

    for s in (0, 1):
        for d in range(4):
            wait_second(s, 1 if d in (0, 2) else 0, d)
        for k in (1, 3):
            assemble(s, k)
        send_third(s, 0, 1)
        send_third(s, 1, 1)
        send_third(s, 1, 3)
    for s in (0, 1):
        for d in range(4):
            got(piece_at(s, 2, d), a2x_send.at[s, d], a2x_got.at[s, d])
        assemble(s, 2)
        send_third(s, 0, 2)
        send_third(s, 0, 3)
        send_third(s, 1, 2)

    for s in (0, 1):
        for way in (0, 1):
            got(r2x.at[s, way], s2x_send.at[s, way], s2x_got.at[s, way])
            k, h = (1, 0) if way == 0 else (3, 1)
            send(close(s, k, h, (r2x.at[s, way],)), r2.at[s, way, h],
                 s2_send.at[s, way, h], s2_got.at[s, way, h], z_dev(1 if way == 0 else 3), pending_sums)

    def nt(lhs, rhs):
        return lax.dot_general(lhs, rhs, (((1,), (1,)), ((), ())), preferred_element_type=F32)

    def weight(ref, b):
        return ref[pl.ds(b * 4, 4)].reshape(BLOCK, HALF)

    def multiply_one(d):
        b = (x + d) % 4
        block = weight(w.at[1], b)
        at = pl.multiple_of(b * BLOCK, 128)
        part = jnp.dot(xv[:, pl.ds(at, BLOCK)], block, preferred_element_type=F32)
        if d == 0:
            keys_sum[...] = part
        else:
            keys_sum[...] += part
        for n in range(BLOCK // TOK):
            rows = pl.ds(pl.multiple_of(b * BLOCK + n * TOK, 128), TOK)
            gnat[rows, :TOK] = nt(kgv[:, HALF:], block[n * TOK:(n + 1) * TOK])

    multiply_one(0)

    for way, k in ((0, 0), (1, 1), (1, 3), (0, 2)):
        for s in (0, 1):
            hand_third(s, way, k)

    def wait_third(s, way):
        for k in (TO_LEFT if way == 0 else TO_RIGHT):
            got(w.at[s, chunk_at(s, 3 if way == 0 else 1, k)], a3_send.at[s, way, k], a3_got.at[s, way, k])

    wait_third(1, 0)
    multiply_one(3)
    wait_third(1, 1)
    multiply_one(1)

    wait_last(0)
    for s in (0, 1):
        for h in (0, 1):
            for way in (0, 1):
                got(r2.at[s, way, h], s2_send.at[s, way, h], s2_got.at[s, way, h])
            rows = pl.ds(h * HROWS, HROWS)
            add_rows(third.at[s, rows], HROWS,
                     [g.at[s, chunk_at(s, 0, 0), rows], r1.at[s, 0, 0, rows], r1.at[s, 1, 0, rows],
                      r2.at[s, 0, h], r2.at[s, 1, h]])
        for j in range(4):
            r3_send[s, j] = pack_rows(third[s, j * ROWS:(j + 1) * ROWS])
        for d in (2, 1, 3):
            send(r3_send.at[s, (first_pos[s] + d) % 4], r3.at[s, d], s3_send.at[s, d], s3_got.at[s, d], first_dev[s](d))

    wait_third(0, 0)
    wait_third(0, 1)
    for s in (0, 1):
        for k in range(4):
            got(w.at[s, chunk_at(s, 2, k)], a3x_send.at[s, k], a3x_got.at[s, k])

    for copy in pending_sums:
        copy.wait_send()
    wnat = g.at[0]

    def unpack(k, _):
        for a in range(4):
            low = a * ROWS - 8 * (a % 2)
            pieces = []
            for b in range(4):
                piece = f32(w[0, b * 4 + k, low:low + ROWS + 8])
                skip = 8 * (a % 2)
                pieces.append(piece[skip:skip + ROWS])
            wnat[a * 4 + k] = jnp.concatenate(pieces, axis=0).astype(BF16)
        return 0
    lax.fori_loop(0, 4, unpack, 0)

    scale = D ** (-0.5)
    multiply_one(2)
    keysv[:, HALF:] = (keys_sum[...] * scale).astype(BF16)

    def multiply_zero(b, _):
        block = weight(wnat, b)
        part = jnp.dot(xv[:, pl.ds(pl.multiple_of(b * BLOCK, 128), BLOCK)], block, preferred_element_type=F32)
        keys_sum[...] += part
        for n in range(BLOCK // TOK):
            at = pl.ds(pl.multiple_of(b * BLOCK + n * TOK, 128), TOK)
            part = gnat[at, :TOK] + nt(kgv[:, :HALF], block[n * TOK:(n + 1) * TOK])
            igv[:, at] = (part * scale).astype(BF16)
        return 0
    keys_sum[...] = jnp.zeros_like(keys_sum)
    lax.fori_loop(0, 4, multiply_zero, 0)
    keysv[:, :HALF] = (keys_sum[...] * scale).astype(BF16)

    for copy in loads[4:]:
        copy.wait()
    other = pl.ds(pl.multiple_of((1 - core) * HALF, 128), HALF)
    got(half_got.at[:, other], o_send.at[2], o_got.at[2])
    half_got[:, mine] = z_got[...]
    outer_grad = half_got[...] * (1.0 / lax.axis_size("rep"))
    momentum_new = outer_mu * ov[...] + outer_grad
    anchor_new = av[...] - outer_rate * (outer_grad + outer_mu * momentum_new)
    momentum_ref[...] = momentum_new
    anchor_ref[...] = anchor_new

    count = jnp.full((1, HALF), step_ref[0].astype(F32), F32)
    fix_first = 1.0 / (1.0 - jnp.exp(count * math.log(beta_first)))
    fix_second = 1.0 / (1.0 - jnp.exp(count * math.log(beta_second)))
    for s in (0, 1):
        at = pl.multiple_of(first_pos[s] * ROWS, 8)
        total = third[s, pl.ds(at, ROWS)]
        for d in (1, 3, 2):
            got(r3.at[s, d], s3_send.at[s, d], s3_got.at[s, d])
            total = total + unpack_rows(r3[s, d])
        gradient = total * scale
        cols = slice(s * HALF, (s + 1) * HALF)
        first_new = beta_first * m1v[:, cols] + (1.0 - beta_first) * gradient
        second_new = beta_second * m2v[:, cols] + (1.0 - beta_second) * gradient * gradient
        direction = first_new * fix_first / (jnp.sqrt(second_new * fix_second) + epsilon)
        local = mv[:, cols]
        stepped = local - inner_rate * (direction + weight_decay * local)
        first_ref[:, cols] = first_new
        second_ref[:, cols] = second_new
        merged_ref[:, cols] = mix_weight * stepped + (1.0 - mix_weight) * anchor_ref[:, cols]

    for copy in pending:
        copy.wait_send()


def exchange(inner_step, *arrays):
    dma = pltpu.SemaphoreType.DMA
    rows = (ROWS, KD)
    return pl.pallas_call(
        kernel,
        out_shape=(
            pltpu.VMEM((TOK, KD), BF16),
            pltpu.VMEM((TOK, D), BF16),
        ) + (pltpu.VMEM(rows, F32),) * 5,
        in_specs=[pl.BlockSpec(memory_space=pl.ANY)] * 8,
        out_specs=(pl.BlockSpec(memory_space=pltpu.VMEM),) * 7,
        scratch_shapes=[
            pltpu.VMEM((TOK, D), BF16),
            pltpu.VMEM((TOK, KD), BF16),
            pltpu.VMEM(rows, F32),
            pltpu.VMEM(rows, F32),
            pltpu.VMEM(rows, F32),
            pltpu.VMEM(rows, F32),
            pltpu.VMEM(rows, F32),
            pltpu.VMEM(rows, F32),
            pltpu.VMEM(rows, F32),
            pltpu.VMEM((ROWS, HALF), F32),
            pltpu.VMEM((ROWS, HALF), F32),
            pltpu.VMEM(rows, F32),
            pltpu.VMEM((2, 16, CHUNK, HALF), BF16),
            pltpu.VMEM((2, 16, CHUNK, HALF), BF16),
            pltpu.VMEM((D, HALF), F32),
            pltpu.VMEM((TOK, HALF), F32),
            pltpu.VMEM((2, 4, 4, 2 * ROWS, HALF // 2), BF16),
            pltpu.VMEM((2, 2, 4, CHUNK, HALF), BF16),
            pltpu.VMEM((2, 2, 2, CHUNK, HALF), BF16),
            pltpu.VMEM((2, 2, 2, HROWS, HALF), BF16),
            pltpu.VMEM((2, 2, HROWS, HALF), BF16),
            pltpu.VMEM((2, CHUNK, HALF), F32),
            pltpu.VMEM((2, 4, 2 * ROWS, HALF // 2), BF16),
            pltpu.VMEM((2, 4, 2 * ROWS, HALF // 2), BF16),
            pltpu.SMEM((1,), jnp.int32),
            dma((8,)), dma((3,)), dma((3,)),
            dma((2, 4)), dma((2, 4)),
            dma((2, 2, 4)), dma((2, 2, 4)), dma((2, 4)), dma((2, 4)),
            dma((2, 2, 4)), dma((2, 2, 4)), dma((2, 4)), dma((2, 4)),
            dma((2, 2, 2)), dma((2, 2, 2)), dma((2, 2, 4)), dma((2, 2, 4)),
            dma((2, 2)), dma((2, 2)), dma((2, 2, 2)), dma((2, 2, 2)), dma((2, 4)), dma((2, 4)),
        ],
        compiler_params=pltpu.CompilerParams(
            collective_id=0, has_side_effects=True, vmem_limit_bytes=56 * 2**20
        ),
        cost_estimate=pl.CostEstimate(
            flops=6 * TOK * D * KD, bytes_accessed=10 * 2**20, transcendentals=0
        ),
        name="exchange",
    )(inner_step, *arrays)


def store_kernel(*refs):
    n = len(refs) // 2
    copies = [pltpu.make_async_copy(refs[i], refs[n + i], refs[-1].at[i]) for i in range(n)]
    for copy in copies:
        copy.start()
    for copy in copies:
        copy.wait()


def store(arrays):
    any_space = pl.BlockSpec(memory_space=pl.ANY)
    return pl.pallas_call(
        store_kernel,
        out_shape=tuple(jax.ShapeDtypeStruct(a.shape, a.dtype) for a in arrays),
        in_specs=[pl.BlockSpec(memory_space=pltpu.VMEM)] * len(arrays),
        out_specs=(any_space,) * len(arrays),
        scratch_shapes=[pltpu.SemaphoreType.DMA((len(arrays),))],
        compiler_params=pltpu.CompilerParams(vmem_limit_bytes=2**20),
        name="store",
    )(*[pltpu.with_memory_space_constraint(a, pltpu.VMEM) for a in arrays])


def body(normed, key_grad, master, first_moment, second_moment, anchor, momentum, inner_step):
    results = exchange(
        inner_step, normed, key_grad, master[0], first_moment[0], second_moment[0], anchor, momentum
    )
    keys, input_grad, merged, first_new, second_new, anchor_new, momentum_new = store(results)
    return (
        keys,
        input_grad,
        merged[None],
        first_new[None],
        second_new[None],
        anchor_new,
        momentum_new,
    )


def solution(mesh):
    in_specs = (
        P(("rep", "fsdp"), None),
        P(("rep", "fsdp"), None),
        P("rep", "fsdp", None),
        P("rep", "fsdp", None),
        P("rep", "fsdp", None),
        P("fsdp", None),
        P("fsdp", None),
        P(),
    )
    out_specs = (
        P(("rep", "fsdp"), None),
        P(("rep", "fsdp"), None),
        P("rep", "fsdp", None),
        P("rep", "fsdp", None),
        P("rep", "fsdp", None),
        P("fsdp", None),
        P("fsdp", None),
    )
    return jax.shard_map(body, mesh=mesh, in_specs=in_specs, out_specs=out_specs, check_vma=False)
```

```python
import math

import jax
import jax.numpy as jnp
from jax import lax
from jax.experimental import pallas as pl
from jax.experimental.pallas import tpu as pltpu
from jax.sharding import PartitionSpec as P

beta_first = 0.9
beta_second = 0.95
inner_rate = 0.1
weight_decay = 0.1
epsilon = 1e-08
outer_rate = 0.7
outer_mu = 0.9
mix_weight = 0.5

MESH = pl.DeviceIdType.MESH
D, KD, TOK = 4608, 1024, 384
ROWS = 72
HALF = KD // 2
CHUNK = 4 * ROWS
HROWS = CHUNK // 2
BLOCK = 4 * CHUNK
TO_RIGHT = (2, 0)
TO_LEFT = (1, 3)
F32, BF16 = jnp.float32, jnp.bfloat16


def f32(v):
    return v.astype(F32)


def kernel(
    step_hbm, normed_hbm, kg_hbm, master_hbm, moment1_hbm, moment2_hbm, anchor_hbm, momentum_hbm,
    keysv, igv, merged_ref, first_ref, second_ref, anchor_ref, momentum_ref,
    xv, kgv, mv, m1v, m2v, av, ov, delta, core_got, half_sum, z_got, half_got,
    w, g, gnat, keys_sum, packed, r1, r1x, r2, r2x, third, r3_send, r3, step_ref,
    load_sem, o_send, o_got,
    f_send, f_got, a2_send, a2_got, a2x_send, a2x_got,
    a3_send, a3_got, a3x_send, a3x_got,
    s1x_send, s1x_got, s1_send, s1_got,
    s2x_send, s2x_got, s2_send, s2_got, s3_send, s3_got,
):
    rep = lax.axis_index("rep")
    shard = lax.axis_index("fsdp")
    x, z, y = shard // 16, (shard // 4) % 4, shard % 4

    def dev(dx, dz, dy):
        return (rep, ((x + dx) % 4) * 16 + ((z + dz) % 4) * 4 + (y + dy) % 4)

    first_pos, last_pos = (x, y), (y, x)
    first_dev = (lambda d: dev(d, 0, 0), lambda d: dev(0, 0, d))
    last_dev = (first_dev[1], first_dev[0])

    def z_dev(d):
        return dev(0, d, 0)

    core = rep % 2
    core_dev = (rep + 1 - 2 * core, shard)
    pair_dev = ((rep + 2) % 4, shard)

    pending = []
    pending_gather = []

    def send(src, dst, ssem, rsem, target, queue=None):
        copy = pltpu.make_async_remote_copy(
            src_ref=src, dst_ref=dst, send_sem=ssem, recv_sem=rsem,
            device_id=target, device_id_type=MESH,
        )
        copy.start()
        (pending if queue is None else queue).append(copy)

    def got(dst, ssem, rsem):
        pltpu.make_async_remote_copy(
            src_ref=dst, dst_ref=dst, send_sem=ssem, recv_sem=rsem,
            device_id=z_dev(1), device_id_type=MESH,
        ).wait_recv()

    loads = [
        pltpu.make_async_copy(master_hbm, mv, load_sem.at[0]),
        pltpu.make_async_copy(normed_hbm, xv, load_sem.at[1]),
        pltpu.make_async_copy(kg_hbm, kgv, load_sem.at[2]),
        pltpu.make_async_copy(anchor_hbm, av, load_sem.at[3]),
        pltpu.make_async_copy(moment1_hbm, m1v, load_sem.at[4]),
        pltpu.make_async_copy(moment2_hbm, m2v, load_sem.at[5]),
        pltpu.make_async_copy(momentum_hbm, ov, load_sem.at[6]),
        pltpu.make_async_copy(step_hbm, step_ref, load_sem.at[7]),
    ]
    for copy in loads:
        copy.start()

    barrier = pltpu.get_barrier_semaphore()
    peers = [first_dev[s](d) for s in (0, 1) for d in (1, 3, 2)] + [z_dev(1), z_dev(3), core_dev, pair_dev]
    for peer in peers:
        pl.semaphore_signal(barrier, inc=1, device_id=peer, device_id_type=MESH)
    pl.semaphore_wait(barrier, len(peers))

    def pack_rows(v):
        return jnp.concatenate([v[:, :HALF // 2], v[:, HALF // 2:]], axis=0).astype(BF16)

    def unpack_rows(v):
        v = f32(v)
        return jnp.concatenate([v[:ROWS], v[ROWS:]], axis=1)

    def piece_at(s, dz, d):
        return packed.at[s, (z + dz) % 4, (first_pos[s] - d) % 4]

    def send_second(s, d):
        here = piece_at(s, 0, d)
        for way, dz in ((0, 1), (1, 3)):
            send(here, here, a2_send.at[s, way, d], a2_got.at[s, way, d], z_dev(dz))

    def wait_second(s, way, d):
        got(piece_at(s, 3 if way == 0 else 1, d), a2_send.at[s, way, d], a2_got.at[s, way, d])

    def hand_second(s, d):
        way = 0 if d in (0, 2) else 1
        wait_second(s, way, d)
        here = piece_at(s, 3 if way == 0 else 1, d)
        send(here, here, a2x_send.at[s, d], a2x_got.at[s, d], z_dev(1 if way == 0 else 3))

    loads[0].wait()
    for s in (0, 1):
        here = piece_at(s, 0, 0)
        here[...] = pack_rows(mv[:, s * HALF:(s + 1) * HALF])
        for d in (1, 3, 2):
            send(here, here, f_send.at[s, d], f_got.at[s, d], first_dev[s](d))
        send_second(s, 0)

    loads[3].wait()
    delta[...] = av[...] - mv[...]
    send(delta, core_got, o_send.at[0], o_got.at[0], core_dev)

    def chunk_at(s, d, k):
        return ((last_pos[s] + d) % 4) * 4 + (z + k) % 4

    def send_relay(s, part, at):
        rows = pl.ds(pl.multiple_of(at, HROWS), HROWS)
        for way, ks in ((0, TO_RIGHT), (1, TO_LEFT)):
            for n, k in enumerate(ks):
                send(g.at[s, chunk_at(s, 2, k), rows], r1x.at[s, way, n, rows],
                     s1x_send.at[s, way, n, part], s1x_got.at[s, way, n, part],
                     last_dev[s](1 if way == 0 else 3))

    def send_one(s, way, k):
        send(g.at[s, chunk_at(s, 1 if way == 0 else 3, k)], r1.at[s, way, k],
             s1_send.at[s, way, k], s1_got.at[s, way, k], last_dev[s](1 if way == 0 else 3))

    loads[1].wait()
    loads[2].wait()

    def tn(lhs, rhs):
        return lax.dot_general(lhs, rhs, (((0,), (0,)), ((), ())), preferred_element_type=F32)

    def grad_block(block):
        def step(i, _):
            at = pl.multiple_of(block * BLOCK + i * TOK, 128)
            part = tn(xv[:, pl.ds(at, TOK)], kgv[...])
            gnat[pl.ds(at, TOK)] = part[:, :HALF]
            flat = g.at[1, pl.ds(block * 4, 4)]
            for n in range(TOK // 96):
                row = i * TOK + n * 96
                rows = pl.ds(pl.multiple_of(row % CHUNK, 96), 96)
                flat[row // CHUNK, rows] = part[n * 96:(n + 1) * 96, HALF:].astype(BF16)
            return 0
        lax.fori_loop(0, BLOCK // TOK, step, 0)

    def pack(block, pair):
        def step(k, _):
            pieces = [
                gnat[pl.ds(pl.multiple_of((2 * pair + a) * BLOCK + k * CHUNK + block * ROWS, 8), ROWS)]
                for a in (0, 1)
            ]
            rows = pl.ds(pl.multiple_of(pair * HROWS, HROWS), HROWS)
            g[0, block * 4 + k, rows] = jnp.concatenate(pieces, axis=0).astype(BF16)
            return 0
        lax.fori_loop(0, 4, step, 0)

    opposite = (x + 2) % 4
    pairs = (opposite // 2, 1 - opposite // 2)
    grad_block(opposite)
    for part in (0, 1):
        send_relay(1, part, part * HROWS)

    got(core_got, o_send.at[0], o_got.at[0])
    mine = pl.ds(pl.multiple_of(core * HALF, 128), HALF)
    half_sum[...] = delta[:, mine] + core_got[:, mine]
    send(half_sum, z_got, o_send.at[1], o_got.at[1], pair_dev)

    grad_block(opposite + 1 - 2 * (opposite % 2))
    pack((y + 2) % 4, pairs[0])
    send_relay(0, 0, pairs[0] * HROWS)

    for d in (1, 3, 2):
        for s in (0, 1):
            got(piece_at(s, 0, d), f_send.at[s, d], f_got.at[s, d])
            send_second(s, d)

    grad_block(x)
    grad_block(x + 1 - 2 * (x % 2))
    pack((y + 2) % 4, pairs[1])
    send_relay(0, 1, pairs[1] * HROWS)
    for d in (1, 3):
        for pair in (0, 1):
            pack((y + d) % 4, pair)
        for s in (1, 0):
            for k in (TO_LEFT if d == 1 else TO_RIGHT):
                send_one(s, 0 if d == 1 else 1, k)
    for pair in (0, 1):
        pack(y, pair)

    def assemble(s, k):
        pieces = [unpack_rows(packed[s, (z + k) % 4, j]) for j in range(4)]
        w[s, chunk_at(s, 0, k)] = jnp.concatenate(pieces, axis=0).astype(BF16)

    def add_rows(dst, rows, sources):
        def step(i, _):
            at = pl.ds(pl.multiple_of(i * 48, 48), 48)
            total = f32(sources[0][at])
            for ref in sources[1:]:
                total = total + f32(ref[at])
            dst[at] = total.astype(dst.dtype)
            return 0
        lax.fori_loop(0, rows // 48, step, 0)

    def hand_on(n):
        for s in (1, 0):
            for way, k in ((0, TO_RIGHT[n]), (1, TO_LEFT[n])):
                for part in (0, 1):
                    at = (part if s == 1 else pairs[part]) * HROWS
                    got(r1x.at[s, way, n, pl.ds(pl.multiple_of(at, HROWS), HROWS)],
                        s1x_send.at[s, way, n, part], s1x_got.at[s, way, n, part])
                here = g.at[s, chunk_at(s, 1 if way == 0 else 3, k)]
                add_rows(here, CHUNK, [here, r1x.at[s, way, n]])
                send_one(s, way, k)

    got(z_got, o_send.at[1], o_got.at[1])
    z_got[...] = half_sum[...] + z_got[...]
    send(z_got, half_got.at[:, mine], o_send.at[2], o_got.at[2], core_dev)

    hand_on(0)
    for d in (0, 1, 3):
        for s in (0, 1):
            hand_second(s, d)
    hand_on(1)
    for s in (0, 1):
        hand_second(s, 2)

    def close(s, k, h, extra=()):
        rows = pl.ds(h * HROWS, HROWS)
        here = g.at[s, chunk_at(s, 0, k), rows]
        add_rows(here, HROWS, [here, r1.at[s, 0, k, rows], r1.at[s, 1, k, rows], *extra])
        return here

    def wait_last(k):
        for s in (0, 1):
            for way in (0, 1):
                got(r1.at[s, way, k], s1_send.at[s, way, k], s1_got.at[s, way, k])

    wait_last(2)
    for s in (0, 1):
        for way in (0, 1):
            send(close(s, 2, way), r2x.at[s, way], s2x_send.at[s, way], s2x_got.at[s, way],
                 z_dev(1 if way == 0 else 3))

    def send_third(s, way, k):
        here = w.at[s, chunk_at(s, 0, k)]
        send(here, here, a3_send.at[s, way, k], a3_got.at[s, way, k], last_dev[s](1 if way == 0 else 3), pending_gather)

    def hand_third(s, way, k):
        here = w.at[s, chunk_at(s, 3 if way == 0 else 1, k)]
        got(here, a3_send.at[s, way, k], a3_got.at[s, way, k])
        send(here, here, a3x_send.at[s, k], a3x_got.at[s, k], last_dev[s](1 if way == 0 else 3), pending_gather)

    for s in (0, 1):
        assemble(s, 0)
        for way in (0, 1):
            send_third(s, way, 0)

    def send_plain_z(s, way):
        k, h = (1, 1) if way == 0 else (3, 0)
        send(close(s, k, h), r2.at[s, way, h], s2_send.at[s, way, h], s2_got.at[s, way, h],
             z_dev(1 if way == 0 else 3))

    wait_last(1)
    for s in (0, 1):
        send_plain_z(s, 0)
    wait_last(3)
    for s in (0, 1):
        send_plain_z(s, 1)

    for s in (0, 1):
        for d in range(4):
            wait_second(s, 1 if d in (0, 2) else 0, d)
        for k in (1, 3):
            assemble(s, k)
        send_third(s, 0, 1)
        send_third(s, 1, 1)
        send_third(s, 1, 3)
    for s in (0, 1):
        for d in range(4):
            got(piece_at(s, 2, d), a2x_send.at[s, d], a2x_got.at[s, d])
        assemble(s, 2)
        send_third(s, 0, 2)
        send_third(s, 0, 3)
        send_third(s, 1, 2)

    for s in (0, 1):
        for way in (0, 1):
            got(r2x.at[s, way], s2x_send.at[s, way], s2x_got.at[s, way])
            k, h = (1, 0) if way == 0 else (3, 1)
            send(close(s, k, h, (r2x.at[s, way],)), r2.at[s, way, h],
                 s2_send.at[s, way, h], s2_got.at[s, way, h], z_dev(1 if way == 0 else 3))

    def nt(lhs, rhs):
        return lax.dot_general(lhs, rhs, (((1,), (1,)), ((), ())), preferred_element_type=F32)

    def weight(ref, b):
        return ref[pl.ds(b * 4, 4)].reshape(BLOCK, HALF)

    def multiply_one(d):
        b = (x + d) % 4
        block = weight(w.at[1], b)
        at = pl.multiple_of(b * BLOCK, 128)
        part = jnp.dot(xv[:, pl.ds(at, BLOCK)], block, preferred_element_type=F32)
        if d == 0:
            keys_sum[...] = part
        else:
            keys_sum[...] += part
        for n in range(BLOCK // TOK):
            rows = pl.ds(pl.multiple_of(b * BLOCK + n * TOK, 128), TOK)
            gnat[rows, :TOK] = nt(kgv[:, HALF:], block[n * TOK:(n + 1) * TOK])

    multiply_one(0)

    for way, k in ((0, 0), (1, 1), (1, 3), (0, 2)):
        for s in (0, 1):
            hand_third(s, way, k)

    def wait_third(s, way):
        for k in (TO_LEFT if way == 0 else TO_RIGHT):
            got(w.at[s, chunk_at(s, 3 if way == 0 else 1, k)], a3_send.at[s, way, k], a3_got.at[s, way, k])

    wait_third(1, 0)
    multiply_one(3)
    wait_third(1, 1)
    multiply_one(1)

    wait_last(0)
    for s in (0, 1):
        for h in (0, 1):
            for way in (0, 1):
                got(r2.at[s, way, h], s2_send.at[s, way, h], s2_got.at[s, way, h])
            rows = pl.ds(h * HROWS, HROWS)
            add_rows(third.at[s, rows], HROWS,
                     [g.at[s, chunk_at(s, 0, 0), rows], r1.at[s, 0, 0, rows], r1.at[s, 1, 0, rows],
                      r2.at[s, 0, h], r2.at[s, 1, h]])
        for j in range(4):
            r3_send[s, j] = pack_rows(third[s, j * ROWS:(j + 1) * ROWS])
        for d in (2, 1, 3):
            send(r3_send.at[s, (first_pos[s] + d) % 4], r3.at[s, d], s3_send.at[s, d], s3_got.at[s, d], first_dev[s](d))

    wait_third(0, 0)
    wait_third(0, 1)
    for s in (0, 1):
        for k in range(4):
            got(w.at[s, chunk_at(s, 2, k)], a3x_send.at[s, k], a3x_got.at[s, k])

    for copy in pending_gather:
        copy.wait_send()

    def unpack(i, _):
        k = i // 4
        cols = pl.ds(pl.multiple_of(i % 4 * 128, 128), 128)
        chunks = [f32(w[0, b * 4 + k, :, cols]) for b in range(4)]
        for a in range(4):
            rows = [chunk[a * ROWS:(a + 1) * ROWS] for chunk in chunks]
            w[0, a * 4 + k, :, cols] = jnp.concatenate(rows, axis=0).astype(BF16)
        return 0
    lax.fori_loop(0, 16, unpack, 0)

    scale = D ** (-0.5)
    multiply_one(2)
    keysv[:, HALF:] = (keys_sum[...] * scale).astype(BF16)

    def multiply_zero(b, _):
        block = weight(w.at[0], b)
        part = jnp.dot(xv[:, pl.ds(pl.multiple_of(b * BLOCK, 128), BLOCK)], block, preferred_element_type=F32)
        keys_sum[...] += part
        for n in range(BLOCK // TOK):
            at = pl.ds(pl.multiple_of(b * BLOCK + n * TOK, 128), TOK)
            part = gnat[at, :TOK] + nt(kgv[:, :HALF], block[n * TOK:(n + 1) * TOK])
            igv[:, at] = (part * scale).astype(BF16)
        return 0
    keys_sum[...] = jnp.zeros_like(keys_sum)
    lax.fori_loop(0, 4, multiply_zero, 0)
    keysv[:, :HALF] = (keys_sum[...] * scale).astype(BF16)

    for copy in loads[4:]:
        copy.wait()
    other = pl.ds(pl.multiple_of((1 - core) * HALF, 128), HALF)
    got(half_got.at[:, other], o_send.at[2], o_got.at[2])
    half_got[:, mine] = z_got[...]
    outer_grad = half_got[...] * (1.0 / lax.axis_size("rep"))
    momentum_new = outer_mu * ov[...] + outer_grad
    anchor_new = av[...] - outer_rate * (outer_grad + outer_mu * momentum_new)
    momentum_ref[...] = momentum_new
    anchor_ref[...] = anchor_new

    count = jnp.full((1, HALF), step_ref[0].astype(F32), F32)
    fix_first = 1.0 / (1.0 - jnp.exp(count * math.log(beta_first)))
    fix_second = 1.0 / (1.0 - jnp.exp(count * math.log(beta_second)))
    for s in (0, 1):
        at = pl.multiple_of(first_pos[s] * ROWS, 8)
        total = third[s, pl.ds(at, ROWS)]
        for d in (1, 3, 2):
            got(r3.at[s, d], s3_send.at[s, d], s3_got.at[s, d])
            total = total + unpack_rows(r3[s, d])
        gradient = total * scale
        cols = slice(s * HALF, (s + 1) * HALF)
        first_new = beta_first * m1v[:, cols] + (1.0 - beta_first) * gradient
        second_new = beta_second * m2v[:, cols] + (1.0 - beta_second) * gradient * gradient
        direction = first_new * fix_first / (jnp.sqrt(second_new * fix_second) + epsilon)
        local = mv[:, cols]
        stepped = local - inner_rate * (direction + weight_decay * local)
        first_ref[:, cols] = first_new
        second_ref[:, cols] = second_new
        merged_ref[:, cols] = mix_weight * stepped + (1.0 - mix_weight) * anchor_ref[:, cols]

    for copy in pending:
        copy.wait_send()


def exchange(inner_step, *arrays):
    dma = pltpu.SemaphoreType.DMA
    rows = (ROWS, KD)
    return pl.pallas_call(
        kernel,
        out_shape=(
            pltpu.VMEM((TOK, KD), BF16),
            pltpu.VMEM((TOK, D), BF16),
        ) + (pltpu.VMEM(rows, F32),) * 5,
        in_specs=[pl.BlockSpec(memory_space=pl.ANY)] * 8,
        out_specs=(pl.BlockSpec(memory_space=pltpu.VMEM),) * 7,
        scratch_shapes=[
            pltpu.VMEM((TOK, D), BF16),
            pltpu.VMEM((TOK, KD), BF16),
            pltpu.VMEM(rows, F32),
            pltpu.VMEM(rows, F32),
            pltpu.VMEM(rows, F32),
            pltpu.VMEM(rows, F32),
            pltpu.VMEM(rows, F32),
            pltpu.VMEM(rows, F32),
            pltpu.VMEM(rows, F32),
            pltpu.VMEM((ROWS, HALF), F32),
            pltpu.VMEM((ROWS, HALF), F32),
            pltpu.VMEM(rows, F32),
            pltpu.VMEM((2, 16, CHUNK, HALF), BF16),
            pltpu.VMEM((2, 16, CHUNK, HALF), BF16),
            pltpu.VMEM((D, HALF), F32),
            pltpu.VMEM((TOK, HALF), F32),
            pltpu.VMEM((2, 4, 4, 2 * ROWS, HALF // 2), BF16),
            pltpu.VMEM((2, 2, 4, CHUNK, HALF), BF16),
            pltpu.VMEM((2, 2, 2, CHUNK, HALF), BF16),
            pltpu.VMEM((2, 2, 2, HROWS, HALF), BF16),
            pltpu.VMEM((2, 2, HROWS, HALF), BF16),
            pltpu.VMEM((2, CHUNK, HALF), F32),
            pltpu.VMEM((2, 4, 2 * ROWS, HALF // 2), BF16),
            pltpu.VMEM((2, 4, 2 * ROWS, HALF // 2), BF16),
            pltpu.SMEM((1,), jnp.int32),
            dma((8,)), dma((3,)), dma((3,)),
            dma((2, 4)), dma((2, 4)),
            dma((2, 2, 4)), dma((2, 2, 4)), dma((2, 4)), dma((2, 4)),
            dma((2, 2, 4)), dma((2, 2, 4)), dma((2, 4)), dma((2, 4)),
            dma((2, 2, 2, 2)), dma((2, 2, 2, 2)), dma((2, 2, 4)), dma((2, 2, 4)),
            dma((2, 2)), dma((2, 2)), dma((2, 2, 2)), dma((2, 2, 2)), dma((2, 4)), dma((2, 4)),
        ],
        compiler_params=pltpu.CompilerParams(
            collective_id=0, has_side_effects=True, vmem_limit_bytes=56 * 2**20
        ),
        cost_estimate=pl.CostEstimate(
            flops=6 * TOK * D * KD, bytes_accessed=10 * 2**20, transcendentals=0
        ),
        name="exchange",
    )(inner_step, *arrays)


def store_kernel(*refs):
    n = len(refs) // 2
    copies = [pltpu.make_async_copy(refs[i], refs[n + i], refs[-1].at[i]) for i in range(n)]
    for copy in copies:
        copy.start()
    for copy in copies:
        copy.wait()


def store(arrays):
    any_space = pl.BlockSpec(memory_space=pl.ANY)
    return pl.pallas_call(
        store_kernel,
        out_shape=tuple(jax.ShapeDtypeStruct(a.shape, a.dtype) for a in arrays),
        in_specs=[pl.BlockSpec(memory_space=pltpu.VMEM)] * len(arrays),
        out_specs=(any_space,) * len(arrays),
        scratch_shapes=[pltpu.SemaphoreType.DMA((len(arrays),))],
        compiler_params=pltpu.CompilerParams(vmem_limit_bytes=2**20),
        name="store",
    )(*[pltpu.with_memory_space_constraint(a, pltpu.VMEM) for a in arrays])


def body(normed, key_grad, master, first_moment, second_moment, anchor, momentum, inner_step):
    results = exchange(
        inner_step, normed, key_grad, master[0], first_moment[0], second_moment[0], anchor, momentum
    )
    keys, input_grad, merged, first_new, second_new, anchor_new, momentum_new = store(results)
    return (
        keys,
        input_grad,
        merged[None],
        first_new[None],
        second_new[None],
        anchor_new,
        momentum_new,
    )


def solution(mesh):
    in_specs = (
        P(("rep", "fsdp"), None),
        P(("rep", "fsdp"), None),
        P("rep", "fsdp", None),
        P("rep", "fsdp", None),
        P("rep", "fsdp", None),
        P("fsdp", None),
        P("fsdp", None),
        P(),
    )
    out_specs = (
        P(("rep", "fsdp"), None),
        P(("rep", "fsdp"), None),
        P("rep", "fsdp", None),
        P("rep", "fsdp", None),
        P("rep", "fsdp", None),
        P("fsdp", None),
        P("fsdp", None),
    )
    return jax.shard_map(body, mesh=mesh, in_specs=in_specs, out_specs=out_specs, check_vma=False)
```

```python
import math

import jax
import jax.numpy as jnp
from jax import lax
from jax.experimental import pallas as pl
from jax.experimental.pallas import tpu as pltpu
from jax.sharding import PartitionSpec as P

beta_first = 0.9
beta_second = 0.95
inner_rate = 0.1
weight_decay = 0.1
epsilon = 1e-08
outer_rate = 0.7
outer_mu = 0.9
mix_weight = 0.5

MESH = pl.DeviceIdType.MESH
D, KD, TOK = 4608, 1024, 384
ROWS = 72
HALF = KD // 2
CHUNK = 4 * ROWS
HROWS = CHUNK // 2
BLOCK = 4 * CHUNK
TO_RIGHT = (2, 0)
TO_LEFT = (1, 3)
F32, BF16 = jnp.float32, jnp.bfloat16


def f32(v):
    return v.astype(F32)


def kernel(
    step_hbm, normed_hbm, kg_hbm, master_hbm, moment1_hbm, moment2_hbm, anchor_hbm, momentum_hbm,
    keysv, igv, merged_ref, first_ref, second_ref, anchor_ref, momentum_ref,
    xv, kgv, mv, m1v, m2v, av, ov, delta, core_got, half_sum, z_got, half_got,
    w, g, gnat, keys_sum, keys_sum0, xp, packed, r1, r1x, r2, r2x, third, r3_send, r3, step_ref,
    load_sem, o_send, o_got,
    f_send, f_got, a2_send, a2_got, a2x_send, a2x_got,
    a3_send, a3_got, a3x_send, a3x_got,
    s1x_send, s1x_got, s1_send, s1_got,
    s2x_send, s2x_got, s2_send, s2_got, s3_send, s3_got,
):
    rep = lax.axis_index("rep")
    shard = lax.axis_index("fsdp")
    x, z, y = shard // 16, (shard // 4) % 4, shard % 4

    def dev(dx, dz, dy):
        return (rep, ((x + dx) % 4) * 16 + ((z + dz) % 4) * 4 + (y + dy) % 4)

    first_pos, last_pos = (x, y), (y, x)
    first_dev = (lambda d: dev(d, 0, 0), lambda d: dev(0, 0, d))
    last_dev = (first_dev[1], first_dev[0])

    def z_dev(d):
        return dev(0, d, 0)

    core = rep % 2
    core_dev = (rep + 1 - 2 * core, shard)
    pair_dev = ((rep + 2) % 4, shard)

    pending = []
    pending_gather = []

    def send(src, dst, ssem, rsem, target, queue=None):
        copy = pltpu.make_async_remote_copy(
            src_ref=src, dst_ref=dst, send_sem=ssem, recv_sem=rsem,
            device_id=target, device_id_type=MESH,
        )
        copy.start()
        (pending if queue is None else queue).append(copy)

    def got(dst, ssem, rsem):
        pltpu.make_async_remote_copy(
            src_ref=dst, dst_ref=dst, send_sem=ssem, recv_sem=rsem,
            device_id=z_dev(1), device_id_type=MESH,
        ).wait_recv()

    loads = [
        pltpu.make_async_copy(master_hbm, mv, load_sem.at[0]),
        pltpu.make_async_copy(normed_hbm, xv, load_sem.at[1]),
        pltpu.make_async_copy(kg_hbm, kgv, load_sem.at[2]),
        pltpu.make_async_copy(anchor_hbm, av, load_sem.at[3]),
        pltpu.make_async_copy(moment1_hbm, m1v, load_sem.at[4]),
        pltpu.make_async_copy(moment2_hbm, m2v, load_sem.at[5]),
        pltpu.make_async_copy(momentum_hbm, ov, load_sem.at[6]),
        pltpu.make_async_copy(step_hbm, step_ref, load_sem.at[7]),
    ]
    for copy in loads:
        copy.start()

    barrier = pltpu.get_barrier_semaphore()
    peers = [first_dev[s](d) for s in (0, 1) for d in (1, 3, 2)] + [z_dev(1), z_dev(3), core_dev, pair_dev]
    for peer in peers:
        pl.semaphore_signal(barrier, inc=1, device_id=peer, device_id_type=MESH)
    pl.semaphore_wait(barrier, len(peers))

    def pack_rows(v):
        return jnp.concatenate([v[:, :HALF // 2], v[:, HALF // 2:]], axis=0).astype(BF16)

    def unpack_rows(v):
        v = f32(v)
        return jnp.concatenate([v[:ROWS], v[ROWS:]], axis=1)

    def piece_at(s, dz, d):
        return packed.at[s, (z + dz) % 4, (first_pos[s] - d) % 4]

    def send_second(s, d):
        here = piece_at(s, 0, d)
        for way, dz in ((0, 1), (1, 3)):
            send(here, here, a2_send.at[s, way, d], a2_got.at[s, way, d], z_dev(dz))

    def wait_second(s, way, d):
        got(piece_at(s, 3 if way == 0 else 1, d), a2_send.at[s, way, d], a2_got.at[s, way, d])

    def hand_second(s, d):
        way = 0 if d in (0, 2) else 1
        wait_second(s, way, d)
        here = piece_at(s, 3 if way == 0 else 1, d)
        send(here, here, a2x_send.at[s, d], a2x_got.at[s, d], z_dev(1 if way == 0 else 3))

    loads[0].wait()
    for s in (0, 1):
        here = piece_at(s, 0, 0)
        here[...] = pack_rows(mv[:, s * HALF:(s + 1) * HALF])
        for d in (1, 3, 2):
            send(here, here, f_send.at[s, d], f_got.at[s, d], first_dev[s](d))
        send_second(s, 0)

    loads[3].wait()
    delta[...] = av[...] - mv[...]
    send(delta, core_got, o_send.at[0], o_got.at[0], core_dev)

    def chunk_at(s, d, k):
        return ((last_pos[s] + d) % 4) * 4 + (z + k) % 4

    def send_relay(s, part, at):
        rows = pl.ds(pl.multiple_of(at, HROWS), HROWS)
        for way, ks in ((0, TO_RIGHT), (1, TO_LEFT)):
            for n, k in enumerate(ks):
                send(g.at[s, chunk_at(s, 2, k), rows], r1x.at[s, way, n, rows],
                     s1x_send.at[s, way, n, part], s1x_got.at[s, way, n, part],
                     last_dev[s](1 if way == 0 else 3))

    def send_one(s, way, k):
        send(g.at[s, chunk_at(s, 1 if way == 0 else 3, k)], r1.at[s, way, k],
             s1_send.at[s, way, k], s1_got.at[s, way, k], last_dev[s](1 if way == 0 else 3))

    loads[1].wait()
    loads[2].wait()

    def tn(lhs, rhs):
        return lax.dot_general(lhs, rhs, (((0,), (0,)), ((), ())), preferred_element_type=F32)

    def grad_block(block):
        def step(i, _):
            at = pl.multiple_of(block * BLOCK + i * TOK, 128)
            part = tn(xv[:, pl.ds(at, TOK)], kgv[...])
            gnat[pl.ds(at, TOK)] = part[:, :HALF]
            flat = g.at[1, pl.ds(block * 4, 4)]
            for n in range(TOK // 96):
                row = i * TOK + n * 96
                rows = pl.ds(pl.multiple_of(row % CHUNK, 96), 96)
                flat[row // CHUNK, rows] = part[n * 96:(n + 1) * 96, HALF:].astype(BF16)
            return 0
        lax.fori_loop(0, BLOCK // TOK, step, 0)

    def pack(block, pair):
        def step(k, _):
            pieces = [
                gnat[pl.ds(pl.multiple_of((2 * pair + a) * BLOCK + k * CHUNK + block * ROWS, 8), ROWS)]
                for a in (0, 1)
            ]
            rows = pl.ds(pl.multiple_of(pair * HROWS, HROWS), HROWS)
            g[0, block * 4 + k, rows] = jnp.concatenate(pieces, axis=0).astype(BF16)
            return 0
        lax.fori_loop(0, 4, step, 0)

    opposite = (x + 2) % 4
    pairs = (opposite // 2, 1 - opposite // 2)
    grad_block(opposite)
    for part in (0, 1):
        send_relay(1, part, part * HROWS)

    got(core_got, o_send.at[0], o_got.at[0])
    mine = pl.ds(pl.multiple_of(core * HALF, 128), HALF)
    half_sum[...] = delta[:, mine] + core_got[:, mine]
    send(half_sum, z_got, o_send.at[1], o_got.at[1], pair_dev)

    grad_block(opposite + 1 - 2 * (opposite % 2))
    pack((y + 2) % 4, pairs[0])
    send_relay(0, 0, pairs[0] * HROWS)

    for d in (1, 3, 2):
        for s in (0, 1):
            got(piece_at(s, 0, d), f_send.at[s, d], f_got.at[s, d])
            send_second(s, d)

    grad_block(x)
    grad_block(x + 1 - 2 * (x % 2))
    pack((y + 2) % 4, pairs[1])
    send_relay(0, 1, pairs[1] * HROWS)
    for d in (1, 3):
        for pair in (0, 1):
            pack((y + d) % 4, pair)
        for s in (1, 0):
            for k in (TO_LEFT if d == 1 else TO_RIGHT):
                send_one(s, 0 if d == 1 else 1, k)
    for pair in (0, 1):
        pack(y, pair)

    def permute(i, _):
        rows = pl.ds(pl.multiple_of(i * 32, 32), 32)
        for b in range(4):
            pieces = []
            for k in range(4):
                for a in range(4):
                    at = a * BLOCK + k * CHUNK + b * ROWS
                    pieces.append(xv[rows, at:at + ROWS])
            xp[rows, b * BLOCK:(b + 1) * BLOCK] = jnp.concatenate(pieces, axis=1)
        return 0

    lax.fori_loop(0, 6, permute, 0)

    def assemble(s, k):
        pieces = [unpack_rows(packed[s, (z + k) % 4, j]) for j in range(4)]
        w[s, chunk_at(s, 0, k)] = jnp.concatenate(pieces, axis=0).astype(BF16)

    def add_rows(dst, rows, sources):
        def step(i, _):
            at = pl.ds(pl.multiple_of(i * 48, 48), 48)
            total = f32(sources[0][at])
            for ref in sources[1:]:
                total = total + f32(ref[at])
            dst[at] = total.astype(dst.dtype)
            return 0
        lax.fori_loop(0, rows // 48, step, 0)

    def hand_on(n):
        for s in (1, 0):
            for way, k in ((0, TO_RIGHT[n]), (1, TO_LEFT[n])):
                for part in (0, 1):
                    at = (part if s == 1 else pairs[part]) * HROWS
                    got(r1x.at[s, way, n, pl.ds(pl.multiple_of(at, HROWS), HROWS)],
                        s1x_send.at[s, way, n, part], s1x_got.at[s, way, n, part])
                here = g.at[s, chunk_at(s, 1 if way == 0 else 3, k)]
                add_rows(here, CHUNK, [here, r1x.at[s, way, n]])
                send_one(s, way, k)

    got(z_got, o_send.at[1], o_got.at[1])
    z_got[...] = half_sum[...] + z_got[...]
    send(z_got, half_got.at[:, mine], o_send.at[2], o_got.at[2], core_dev)

    hand_on(0)
    for d in (0, 1, 3):
        for s in (0, 1):
            hand_second(s, d)
    hand_on(1)
    for s in (0, 1):
        hand_second(s, 2)

    def close(s, k, h, extra=()):
        rows = pl.ds(h * HROWS, HROWS)
        here = g.at[s, chunk_at(s, 0, k), rows]
        add_rows(here, HROWS, [here, r1.at[s, 0, k, rows], r1.at[s, 1, k, rows], *extra])
        return here

    def wait_last(k):
        for s in (0, 1):
            for way in (0, 1):
                got(r1.at[s, way, k], s1_send.at[s, way, k], s1_got.at[s, way, k])

    lax.fori_loop(6, TOK // 32, permute, 0)
    wait_last(2)
    for s in (0, 1):
        for way in (0, 1):
            send(close(s, 2, way), r2x.at[s, way], s2x_send.at[s, way], s2x_got.at[s, way],
                 z_dev(1 if way == 0 else 3))

    def send_third(s, way, k):
        here = w.at[s, chunk_at(s, 0, k)]
        send(here, here, a3_send.at[s, way, k], a3_got.at[s, way, k], last_dev[s](1 if way == 0 else 3), pending_gather)

    def hand_third(s, way, k):
        here = w.at[s, chunk_at(s, 3 if way == 0 else 1, k)]
        got(here, a3_send.at[s, way, k], a3_got.at[s, way, k])
        send(here, here, a3x_send.at[s, k], a3x_got.at[s, k], last_dev[s](1 if way == 0 else 3), pending_gather)

    for s in (0, 1):
        assemble(s, 0)
        for way in (0, 1):
            send_third(s, way, 0)

    def send_plain_z(s, way):
        k, h = (1, 1) if way == 0 else (3, 0)
        send(close(s, k, h), r2.at[s, way, h], s2_send.at[s, way, h], s2_got.at[s, way, h],
             z_dev(1 if way == 0 else 3))

    wait_last(1)
    for s in (0, 1):
        send_plain_z(s, 0)
    wait_last(3)
    for s in (0, 1):
        send_plain_z(s, 1)

    for s in (0, 1):
        for d in range(4):
            wait_second(s, 1 if d in (0, 2) else 0, d)
        for k in (1, 3):
            assemble(s, k)
        send_third(s, 0, 1)
        send_third(s, 1, 1)
        send_third(s, 1, 3)
    for s in (0, 1):
        for d in range(4):
            got(piece_at(s, 2, d), a2x_send.at[s, d], a2x_got.at[s, d])
        assemble(s, 2)
        send_third(s, 0, 2)
        send_third(s, 0, 3)
        send_third(s, 1, 2)

    for s in (0, 1):
        for way in (0, 1):
            got(r2x.at[s, way], s2x_send.at[s, way], s2x_got.at[s, way])
            k, h = (1, 0) if way == 0 else (3, 1)
            send(close(s, k, h, (r2x.at[s, way],)), r2.at[s, way, h],
                 s2_send.at[s, way, h], s2_got.at[s, way, h], z_dev(1 if way == 0 else 3))

    def nt(lhs, rhs):
        return lax.dot_general(lhs, rhs, (((1,), (1,)), ((), ())), preferred_element_type=F32)

    def weight(ref, b):
        return ref[pl.ds(b * 4, 4)].reshape(BLOCK, HALF)

    def multiply_one(d):
        b = (x + d) % 4
        block = weight(w.at[1], b)
        at = pl.multiple_of(b * BLOCK, 128)
        part = jnp.dot(xv[:, pl.ds(at, BLOCK)], block, preferred_element_type=F32)
        if d == 0:
            keys_sum[...] = part
        else:
            keys_sum[...] += part
        for n in range(BLOCK // TOK):
            rows = pl.ds(pl.multiple_of(b * BLOCK + n * TOK, 128), TOK)
            gnat[rows, :TOK] = nt(kgv[:, HALF:], block[n * TOK:(n + 1) * TOK])


    for way, k in ((0, 0), (1, 1), (1, 3), (0, 2)):
        for s in (0, 1):
            hand_third(s, way, k)

    def multiply_keys(d):
        b = (y + d) % 4
        at = pl.multiple_of(b * BLOCK, 128)
        part = jnp.dot(xp[:, pl.ds(at, BLOCK)], weight(w.at[0], b), preferred_element_type=F32)
        if d == 0:
            keys_sum0[...] = part
        else:
            keys_sum0[...] += part

    multiply_one(0)
    multiply_keys(0)

    def wait_third(s, way):
        for k in (TO_LEFT if way == 0 else TO_RIGHT):
            got(w.at[s, chunk_at(s, 3 if way == 0 else 1, k)], a3_send.at[s, way, k], a3_got.at[s, way, k])

    wait_third(1, 0)
    multiply_one(3)
    wait_third(1, 1)
    multiply_one(1)
    wait_third(0, 0)
    multiply_keys(3)
    wait_third(0, 1)
    multiply_keys(1)

    wait_last(0)
    for s in (0, 1):
        for h in (0, 1):
            for way in (0, 1):
                got(r2.at[s, way, h], s2_send.at[s, way, h], s2_got.at[s, way, h])
            rows = pl.ds(h * HROWS, HROWS)
            add_rows(third.at[s, rows], HROWS,
                     [g.at[s, chunk_at(s, 0, 0), rows], r1.at[s, 0, 0, rows], r1.at[s, 1, 0, rows],
                      r2.at[s, 0, h], r2.at[s, 1, h]])
        for j in range(4):
            r3_send[s, j] = pack_rows(third[s, j * ROWS:(j + 1) * ROWS])
        for d in (2, 1, 3):
            send(r3_send.at[s, (first_pos[s] + d) % 4], r3.at[s, d], s3_send.at[s, d], s3_got.at[s, d], first_dev[s](d))

    for k in range(4):
        got(w.at[1, chunk_at(1, 2, k)], a3x_send.at[1, k], a3x_got.at[1, k])
    multiply_one(2)
    for k in range(4):
        got(w.at[0, chunk_at(0, 2, k)], a3x_send.at[0, k], a3x_got.at[0, k])
    multiply_keys(2)

    for copy in pending_gather:
        copy.wait_send()

    def unpack(i, _):
        k = i // 4
        cols = pl.ds(pl.multiple_of(i % 4 * 128, 128), 128)
        chunks = [f32(w[0, b * 4 + k, :, cols]) for b in range(4)]
        for a in range(4):
            rows = [chunk[a * ROWS:(a + 1) * ROWS] for chunk in chunks]
            w[0, a * 4 + k, :, cols] = jnp.concatenate(rows, axis=0).astype(BF16)
        return 0
    lax.fori_loop(0, 16, unpack, 0)

    scale = D ** (-0.5)
    keysv[:, HALF:] = (keys_sum[...] * scale).astype(BF16)

    def multiply_zero(b, _):
        block = weight(w.at[0], b)
        for n in range(BLOCK // TOK):
            at = pl.ds(pl.multiple_of(b * BLOCK + n * TOK, 128), TOK)
            part = gnat[at, :TOK] + nt(kgv[:, :HALF], block[n * TOK:(n + 1) * TOK])
            igv[:, at] = (part * scale).astype(BF16)
        return 0
    lax.fori_loop(0, 4, multiply_zero, 0)
    keysv[:, :HALF] = (keys_sum0[...] * scale).astype(BF16)

    for copy in loads[4:]:
        copy.wait()
    other = pl.ds(pl.multiple_of((1 - core) * HALF, 128), HALF)
    got(half_got.at[:, other], o_send.at[2], o_got.at[2])
    half_got[:, mine] = z_got[...]
    outer_grad = half_got[...] * (1.0 / lax.axis_size("rep"))
    momentum_new = outer_mu * ov[...] + outer_grad
    anchor_new = av[...] - outer_rate * (outer_grad + outer_mu * momentum_new)
    momentum_ref[...] = momentum_new
    anchor_ref[...] = anchor_new

    count = jnp.full((1, HALF), step_ref[0].astype(F32), F32)
    fix_first = 1.0 / (1.0 - jnp.exp(count * math.log(beta_first)))
    fix_second = 1.0 / (1.0 - jnp.exp(count * math.log(beta_second)))
    for s in (0, 1):
        at = pl.multiple_of(first_pos[s] * ROWS, 8)
        total = third[s, pl.ds(at, ROWS)]
        for d in (1, 3, 2):
            got(r3.at[s, d], s3_send.at[s, d], s3_got.at[s, d])
            total = total + unpack_rows(r3[s, d])
        gradient = total * scale
        cols = slice(s * HALF, (s + 1) * HALF)
        first_new = beta_first * m1v[:, cols] + (1.0 - beta_first) * gradient
        second_new = beta_second * m2v[:, cols] + (1.0 - beta_second) * gradient * gradient
        direction = first_new * fix_first / (jnp.sqrt(second_new * fix_second) + epsilon)
        local = mv[:, cols]
        stepped = local - inner_rate * (direction + weight_decay * local)
        first_ref[:, cols] = first_new
        second_ref[:, cols] = second_new
        merged_ref[:, cols] = mix_weight * stepped + (1.0 - mix_weight) * anchor_ref[:, cols]

    for copy in pending:
        copy.wait_send()


def exchange(inner_step, *arrays):
    dma = pltpu.SemaphoreType.DMA
    rows = (ROWS, KD)
    return pl.pallas_call(
        kernel,
        out_shape=(
            pltpu.VMEM((TOK, KD), BF16),
            pltpu.VMEM((TOK, D), BF16),
        ) + (pltpu.VMEM(rows, F32),) * 5,
        in_specs=[pl.BlockSpec(memory_space=pl.ANY)] * 8,
        out_specs=(pl.BlockSpec(memory_space=pltpu.VMEM),) * 7,
        scratch_shapes=[
            pltpu.VMEM((TOK, D), BF16),
            pltpu.VMEM((TOK, KD), BF16),
            pltpu.VMEM(rows, F32),
            pltpu.VMEM(rows, F32),
            pltpu.VMEM(rows, F32),
            pltpu.VMEM(rows, F32),
            pltpu.VMEM(rows, F32),
            pltpu.VMEM(rows, F32),
            pltpu.VMEM(rows, F32),
            pltpu.VMEM((ROWS, HALF), F32),
            pltpu.VMEM((ROWS, HALF), F32),
            pltpu.VMEM(rows, F32),
            pltpu.VMEM((2, 16, CHUNK, HALF), BF16),
            pltpu.VMEM((2, 16, CHUNK, HALF), BF16),
            pltpu.VMEM((D, HALF), F32),
            pltpu.VMEM((TOK, HALF), F32),
            pltpu.VMEM((TOK, HALF), F32),
            pltpu.VMEM((TOK, D), BF16),
            pltpu.VMEM((2, 4, 4, 2 * ROWS, HALF // 2), BF16),
            pltpu.VMEM((2, 2, 4, CHUNK, HALF), BF16),
            pltpu.VMEM((2, 2, 2, CHUNK, HALF), BF16),
            pltpu.VMEM((2, 2, 2, HROWS, HALF), BF16),
            pltpu.VMEM((2, 2, HROWS, HALF), BF16),
            pltpu.VMEM((2, CHUNK, HALF), F32),
            pltpu.VMEM((2, 4, 2 * ROWS, HALF // 2), BF16),
            pltpu.VMEM((2, 4, 2 * ROWS, HALF // 2), BF16),
            pltpu.SMEM((1,), jnp.int32),
            dma((8,)), dma((3,)), dma((3,)),
            dma((2, 4)), dma((2, 4)),
            dma((2, 2, 4)), dma((2, 2, 4)), dma((2, 4)), dma((2, 4)),
            dma((2, 2, 4)), dma((2, 2, 4)), dma((2, 4)), dma((2, 4)),
            dma((2, 2, 2, 2)), dma((2, 2, 2, 2)), dma((2, 2, 4)), dma((2, 2, 4)),
            dma((2, 2)), dma((2, 2)), dma((2, 2, 2)), dma((2, 2, 2)), dma((2, 4)), dma((2, 4)),
        ],
        compiler_params=pltpu.CompilerParams(
            collective_id=0, has_side_effects=True, vmem_limit_bytes=56 * 2**20
        ),
        cost_estimate=pl.CostEstimate(
            flops=6 * TOK * D * KD, bytes_accessed=10 * 2**20, transcendentals=0
        ),
        name="exchange",
    )(inner_step, *arrays)


def store_kernel(*refs):
    n = len(refs) // 2
    copies = [pltpu.make_async_copy(refs[i], refs[n + i], refs[-1].at[i]) for i in range(n)]
    for copy in copies:
        copy.start()
    for copy in copies:
        copy.wait()


def store(arrays):
    any_space = pl.BlockSpec(memory_space=pl.ANY)
    return pl.pallas_call(
        store_kernel,
        out_shape=tuple(jax.ShapeDtypeStruct(a.shape, a.dtype) for a in arrays),
        in_specs=[pl.BlockSpec(memory_space=pltpu.VMEM)] * len(arrays),
        out_specs=(any_space,) * len(arrays),
        scratch_shapes=[pltpu.SemaphoreType.DMA((len(arrays),))],
        compiler_params=pltpu.CompilerParams(vmem_limit_bytes=2**20),
        name="store",
    )(*[pltpu.with_memory_space_constraint(a, pltpu.VMEM) for a in arrays])


def body(normed, key_grad, master, first_moment, second_moment, anchor, momentum, inner_step):
    results = exchange(
        inner_step, normed, key_grad, master[0], first_moment[0], second_moment[0], anchor, momentum
    )
    keys, input_grad, merged, first_new, second_new, anchor_new, momentum_new = store(results)
    return (
        keys,
        input_grad,
        merged[None],
        first_new[None],
        second_new[None],
        anchor_new,
        momentum_new,
    )


def solution(mesh):
    in_specs = (
        P(("rep", "fsdp"), None),
        P(("rep", "fsdp"), None),
        P("rep", "fsdp", None),
        P("rep", "fsdp", None),
        P("rep", "fsdp", None),
        P("fsdp", None),
        P("fsdp", None),
        P(),
    )
    out_specs = (
        P(("rep", "fsdp"), None),
        P(("rep", "fsdp"), None),
        P("rep", "fsdp", None),
        P("rep", "fsdp", None),
        P("rep", "fsdp", None),
        P("fsdp", None),
        P("fsdp", None),
    )
    return jax.shard_map(body, mesh=mesh, in_specs=in_specs, out_specs=out_specs, check_vma=False)
```

```python
import math

import jax
import jax.numpy as jnp
from jax import lax
from jax.experimental import pallas as pl
from jax.experimental.pallas import tpu as pltpu
from jax.sharding import PartitionSpec as P

beta_first = 0.9
beta_second = 0.95
inner_rate = 0.1
weight_decay = 0.1
epsilon = 1e-08
outer_rate = 0.7
outer_mu = 0.9
mix_weight = 0.5

MESH = pl.DeviceIdType.MESH
D, KD, TOK = 4608, 1024, 384
ROWS = 72
HALF = KD // 2
CHUNK = 4 * ROWS
HROWS = CHUNK // 2
BLOCK = 4 * CHUNK
TO_RIGHT = (2, 0)
TO_LEFT = (1, 3)
F32, BF16 = jnp.float32, jnp.bfloat16


def f32(v):
    return v.astype(F32)


def kernel(
    step_hbm, normed_hbm, kg_hbm, master_hbm, moment1_hbm, moment2_hbm, anchor_hbm, momentum_hbm,
    keysv, igv, merged_ref, first_ref, second_ref, anchor_ref, momentum_ref,
    xv, kgv, mv, m1v, m2v, av, ov, delta, core_got, half_sum, z_got, half_got,
    w, g, gnat, keys_sum, keys_sum0, xp, packed, r1, r1x, r2, r2x, third, r3_send, r3, step_ref,
    load_sem, o_send, o_got,
    f_send, f_got, a2_send, a2_got, a2x_send, a2x_got,
    a3_send, a3_got, a3x_send, a3x_got,
    s1x_send, s1x_got, s1_send, s1_got,
    s2x_send, s2x_got, s2_send, s2_got, s3_send, s3_got,
):
    rep = lax.axis_index("rep")
    shard = lax.axis_index("fsdp")
    x, z, y = shard // 16, (shard // 4) % 4, shard % 4

    def dev(dx, dz, dy):
        return (rep, ((x + dx) % 4) * 16 + ((z + dz) % 4) * 4 + (y + dy) % 4)

    first_pos, last_pos = (x, y), (y, x)
    first_dev = (lambda d: dev(d, 0, 0), lambda d: dev(0, 0, d))
    last_dev = (first_dev[1], first_dev[0])

    def z_dev(d):
        return dev(0, d, 0)

    core = rep % 2
    core_dev = (rep + 1 - 2 * core, shard)
    pair_dev = ((rep + 2) % 4, shard)

    pending = []
    pending_gather = []

    def send(src, dst, ssem, rsem, target, queue=None):
        copy = pltpu.make_async_remote_copy(
            src_ref=src, dst_ref=dst, send_sem=ssem, recv_sem=rsem,
            device_id=target, device_id_type=MESH,
        )
        copy.start()
        (pending if queue is None else queue).append(copy)

    def got(dst, ssem, rsem):
        pltpu.make_async_remote_copy(
            src_ref=dst, dst_ref=dst, send_sem=ssem, recv_sem=rsem,
            device_id=z_dev(1), device_id_type=MESH,
        ).wait_recv()

    loads = [
        pltpu.make_async_copy(master_hbm, mv, load_sem.at[0]),
        pltpu.make_async_copy(normed_hbm, xv, load_sem.at[1]),
        pltpu.make_async_copy(kg_hbm, kgv, load_sem.at[2]),
        pltpu.make_async_copy(anchor_hbm, av, load_sem.at[3]),
        pltpu.make_async_copy(moment1_hbm, m1v, load_sem.at[4]),
        pltpu.make_async_copy(moment2_hbm, m2v, load_sem.at[5]),
        pltpu.make_async_copy(momentum_hbm, ov, load_sem.at[6]),
        pltpu.make_async_copy(step_hbm, step_ref, load_sem.at[7]),
    ]
    for copy in loads:
        copy.start()

    barrier = pltpu.get_barrier_semaphore()
    peers = [first_dev[s](d) for s in (0, 1) for d in (1, 3, 2)] + [z_dev(1), z_dev(3), core_dev, pair_dev]
    for peer in peers:
        pl.semaphore_signal(barrier, inc=1, device_id=peer, device_id_type=MESH)
    pl.semaphore_wait(barrier, len(peers))

    def pack_rows(v):
        return jnp.concatenate([v[:, :HALF // 2], v[:, HALF // 2:]], axis=0).astype(BF16)

    def unpack_rows(v):
        v = f32(v)
        return jnp.concatenate([v[:ROWS], v[ROWS:]], axis=1)

    def piece_at(s, dz, d):
        return packed.at[s, (z + dz) % 4, (first_pos[s] - d) % 4]

    def send_second(s, d):
        here = piece_at(s, 0, d)
        for way, dz in ((0, 1), (1, 3)):
            send(here, here, a2_send.at[s, way, d], a2_got.at[s, way, d], z_dev(dz))

    def wait_second(s, way, d):
        got(piece_at(s, 3 if way == 0 else 1, d), a2_send.at[s, way, d], a2_got.at[s, way, d])

    def hand_second(s, d):
        way = 0 if d in (0, 2) else 1
        wait_second(s, way, d)
        here = piece_at(s, 3 if way == 0 else 1, d)
        send(here, here, a2x_send.at[s, d], a2x_got.at[s, d], z_dev(1 if way == 0 else 3))

    loads[0].wait()
    for s in (0, 1):
        here = piece_at(s, 0, 0)
        here[...] = pack_rows(mv[:, s * HALF:(s + 1) * HALF])
        for d in (1, 3, 2):
            send(here, here, f_send.at[s, d], f_got.at[s, d], first_dev[s](d))
        send_second(s, 0)

    loads[3].wait()
    delta[...] = av[...] - mv[...]
    send(delta, core_got, o_send.at[0], o_got.at[0], core_dev)

    def chunk_at(s, d, k):
        return ((last_pos[s] + d) % 4) * 4 + (z + k) % 4

    def send_relay(s, part, at):
        rows = pl.ds(pl.multiple_of(at, HROWS), HROWS)
        for way, ks in ((0, TO_RIGHT), (1, TO_LEFT)):
            for n, k in enumerate(ks):
                send(g.at[s, chunk_at(s, 2, k), rows], r1x.at[s, way, n, rows],
                     s1x_send.at[s, way, n, part], s1x_got.at[s, way, n, part],
                     last_dev[s](1 if way == 0 else 3))

    def send_one(s, way, k):
        send(g.at[s, chunk_at(s, 1 if way == 0 else 3, k)], r1.at[s, way, k],
             s1_send.at[s, way, k], s1_got.at[s, way, k], last_dev[s](1 if way == 0 else 3))

    loads[1].wait()
    loads[2].wait()

    def tn(lhs, rhs):
        return lax.dot_general(lhs, rhs, (((0,), (0,)), ((), ())), preferred_element_type=F32)

    def grad_block(block):
        def step(i, _):
            at = pl.multiple_of(block * BLOCK + i * TOK, 128)
            part = tn(xv[:, pl.ds(at, TOK)], kgv[...])
            gnat[pl.ds(at, TOK)] = part[:, :HALF]
            flat = g.at[1, pl.ds(block * 4, 4)]
            for n in range(TOK // 96):
                row = i * TOK + n * 96
                rows = pl.ds(pl.multiple_of(row % CHUNK, 96), 96)
                flat[row // CHUNK, rows] = part[n * 96:(n + 1) * 96, HALF:].astype(BF16)
            return 0
        lax.fori_loop(0, BLOCK // TOK, step, 0)

    def pack(block, pair):
        def step(k, _):
            pieces = [
                gnat[pl.ds(pl.multiple_of((2 * pair + a) * BLOCK + k * CHUNK + block * ROWS, 8), ROWS)]
                for a in (0, 1)
            ]
            rows = pl.ds(pl.multiple_of(pair * HROWS, HROWS), HROWS)
            g[0, block * 4 + k, rows] = jnp.concatenate(pieces, axis=0).astype(BF16)
            return 0
        lax.fori_loop(0, 4, step, 0)

    opposite = (x + 2) % 4
    pairs = (opposite // 2, 1 - opposite // 2)
    grad_block(opposite)
    for part in (0, 1):
        send_relay(1, part, part * HROWS)

    got(core_got, o_send.at[0], o_got.at[0])
    mine = pl.ds(pl.multiple_of(core * HALF, 128), HALF)
    half_sum[...] = delta[:, mine] + core_got[:, mine]
    send(half_sum, z_got, o_send.at[1], o_got.at[1], pair_dev)

    grad_block(opposite + 1 - 2 * (opposite % 2))
    pack((y + 2) % 4, pairs[0])
    send_relay(0, 0, pairs[0] * HROWS)

    for d in (1, 3, 2):
        for s in (0, 1):
            got(piece_at(s, 0, d), f_send.at[s, d], f_got.at[s, d])
            send_second(s, d)

    grad_block(x)
    grad_block(x + 1 - 2 * (x % 2))
    pack((y + 2) % 4, pairs[1])
    send_relay(0, 1, pairs[1] * HROWS)
    for d in (1, 3):
        for pair in (0, 1):
            pack((y + d) % 4, pair)
        for s in (1, 0):
            for k in (TO_LEFT if d == 1 else TO_RIGHT):
                send_one(s, 0 if d == 1 else 1, k)
    for pair in (0, 1):
        pack(y, pair)

    def permute(i, _):
        rows = pl.ds(pl.multiple_of(i * 32, 32), 32)
        for b in range(4):
            pieces = []
            for k in range(4):
                for a in range(4):
                    at = a * BLOCK + k * CHUNK + b * ROWS
                    pieces.append(xv[rows, at:at + ROWS])
            xp[rows, b * BLOCK:(b + 1) * BLOCK] = jnp.concatenate(pieces, axis=1)
        return 0

    lax.fori_loop(0, 6, permute, 0)

    def assemble(s, k):
        pieces = [unpack_rows(packed[s, (z + k) % 4, j]) for j in range(4)]
        w[s, chunk_at(s, 0, k)] = jnp.concatenate(pieces, axis=0).astype(BF16)

    def add_rows(dst, rows, sources):
        def step(i, _):
            at = pl.ds(pl.multiple_of(i * 48, 48), 48)
            total = f32(sources[0][at])
            for ref in sources[1:]:
                total = total + f32(ref[at])
            dst[at] = total.astype(dst.dtype)
            return 0
        lax.fori_loop(0, rows // 48, step, 0)

    def hand_on(n):
        for s in (1, 0):
            for way, k in ((0, TO_RIGHT[n]), (1, TO_LEFT[n])):
                for part in (0, 1):
                    at = (part if s == 1 else pairs[part]) * HROWS
                    got(r1x.at[s, way, n, pl.ds(pl.multiple_of(at, HROWS), HROWS)],
                        s1x_send.at[s, way, n, part], s1x_got.at[s, way, n, part])
                here = g.at[s, chunk_at(s, 1 if way == 0 else 3, k)]
                add_rows(here, CHUNK, [here, r1x.at[s, way, n]])
                send_one(s, way, k)

    got(z_got, o_send.at[1], o_got.at[1])
    z_got[...] = half_sum[...] + z_got[...]
    send(z_got, half_got.at[:, mine], o_send.at[2], o_got.at[2], core_dev)

    hand_on(0)
    for d in (0, 1, 3):
        for s in (0, 1):
            hand_second(s, d)
    hand_on(1)
    for s in (0, 1):
        hand_second(s, 2)

    def close(s, k, h, extra=()):
        rows = pl.ds(h * HROWS, HROWS)
        here = g.at[s, chunk_at(s, 0, k), rows]
        add_rows(here, HROWS, [here, r1.at[s, 0, k, rows], r1.at[s, 1, k, rows], *extra])
        return here

    def wait_last(k):
        for s in (0, 1):
            for way in (0, 1):
                got(r1.at[s, way, k], s1_send.at[s, way, k], s1_got.at[s, way, k])

    lax.fori_loop(6, TOK // 32, permute, 0)
    wait_last(2)
    for s in (0, 1):
        for way in (0, 1):
            send(close(s, 2, way), r2x.at[s, way], s2x_send.at[s, way], s2x_got.at[s, way],
                 z_dev(1 if way == 0 else 3))

    def send_third(s, way, k):
        here = w.at[s, chunk_at(s, 0, k)]
        send(here, here, a3_send.at[s, way, k], a3_got.at[s, way, k], last_dev[s](1 if way == 0 else 3), pending_gather)

    def hand_third(s, way, k):
        here = w.at[s, chunk_at(s, 3 if way == 0 else 1, k)]
        got(here, a3_send.at[s, way, k], a3_got.at[s, way, k])
        send(here, here, a3x_send.at[s, k], a3x_got.at[s, k], last_dev[s](1 if way == 0 else 3), pending_gather)

    for s in (0, 1):
        assemble(s, 0)
        for way in (0, 1):
            send_third(s, way, 0)

    def send_plain_z(s, way):
        k, h = (1, 1) if way == 0 else (3, 0)
        send(close(s, k, h), r2.at[s, way, h], s2_send.at[s, way, h], s2_got.at[s, way, h],
             z_dev(1 if way == 0 else 3))

    wait_last(1)
    for s in (0, 1):
        send_plain_z(s, 0)
    wait_last(3)
    for s in (0, 1):
        send_plain_z(s, 1)

    for s in (0, 1):
        for d in range(4):
            wait_second(s, 1 if d in (0, 2) else 0, d)
        for k in (1, 3):
            assemble(s, k)
        send_third(s, 0, 1)
        send_third(s, 1, 1)
        send_third(s, 1, 3)
    for s in (0, 1):
        for d in range(4):
            got(piece_at(s, 2, d), a2x_send.at[s, d], a2x_got.at[s, d])
        assemble(s, 2)
        send_third(s, 0, 2)
        send_third(s, 0, 3)
        send_third(s, 1, 2)

    for s in (0, 1):
        for way in (0, 1):
            got(r2x.at[s, way], s2x_send.at[s, way], s2x_got.at[s, way])
            k, h = (1, 0) if way == 0 else (3, 1)
            send(close(s, k, h, (r2x.at[s, way],)), r2.at[s, way, h],
                 s2_send.at[s, way, h], s2_got.at[s, way, h], z_dev(1 if way == 0 else 3))

    def nt(lhs, rhs):
        return lax.dot_general(lhs, rhs, (((1,), (1,)), ((), ())), preferred_element_type=F32)

    def weight(ref, b):
        return ref[pl.ds(b * 4, 4)].reshape(BLOCK, HALF)

    def multiply_one(d):
        b = (x + d) % 4
        block = weight(w.at[1], b)
        at = pl.multiple_of(b * BLOCK, 128)
        part = jnp.dot(xv[:, pl.ds(at, BLOCK)], block, preferred_element_type=F32)
        if d == 0:
            keys_sum[...] = part
        else:
            keys_sum[...] += part
        for n in range(BLOCK // TOK):
            rows = pl.ds(pl.multiple_of(b * BLOCK + n * TOK, 128), TOK)
            gnat[rows, :TOK] = nt(kgv[:, HALF:], block[n * TOK:(n + 1) * TOK])


    for way, k in ((0, 0), (1, 1), (1, 3), (0, 2)):
        for s in (0, 1):
            hand_third(s, way, k)

    def multiply_keys(d):
        b = (y + d) % 4
        at = pl.multiple_of(b * BLOCK, 128)
        part = jnp.dot(xp[:, pl.ds(at, BLOCK)], weight(w.at[0], b), preferred_element_type=F32)
        if d == 0:
            keys_sum0[...] = part
        else:
            keys_sum0[...] += part

    multiply_one(0)
    multiply_keys(0)

    def wait_third(s, way):
        for k in (TO_LEFT if way == 0 else TO_RIGHT):
            got(w.at[s, chunk_at(s, 3 if way == 0 else 1, k)], a3_send.at[s, way, k], a3_got.at[s, way, k])

    wait_third(1, 0)
    multiply_one(3)
    wait_third(1, 1)
    multiply_one(1)
    wait_third(0, 0)
    multiply_keys(3)
    wait_third(0, 1)
    multiply_keys(1)

    for k in range(4):
        got(w.at[1, chunk_at(1, 2, k)], a3x_send.at[1, k], a3x_got.at[1, k])
    multiply_one(2)
    wait_last(0)
    for s in (0, 1):
        for h in (0, 1):
            for way in (0, 1):
                got(r2.at[s, way, h], s2_send.at[s, way, h], s2_got.at[s, way, h])
            rows = pl.ds(h * HROWS, HROWS)
            add_rows(third.at[s, rows], HROWS,
                     [g.at[s, chunk_at(s, 0, 0), rows], r1.at[s, 0, 0, rows], r1.at[s, 1, 0, rows],
                      r2.at[s, 0, h], r2.at[s, 1, h]])
        for j in range(4):
            r3_send[s, j] = pack_rows(third[s, j * ROWS:(j + 1) * ROWS])
        for d in (2, 1, 3):
            send(r3_send.at[s, (first_pos[s] + d) % 4], r3.at[s, d], s3_send.at[s, d], s3_got.at[s, d], first_dev[s](d))

    for k in range(4):
        got(w.at[0, chunk_at(0, 2, k)], a3x_send.at[0, k], a3x_got.at[0, k])
    multiply_keys(2)

    for copy in pending_gather:
        copy.wait_send()

    def unpack(i, _):
        k = i // 4
        cols = pl.ds(pl.multiple_of(i % 4 * 128, 128), 128)
        chunks = [f32(w[0, b * 4 + k, :, cols]) for b in range(4)]
        for a in range(4):
            rows = [chunk[a * ROWS:(a + 1) * ROWS] for chunk in chunks]
            w[0, a * 4 + k, :, cols] = jnp.concatenate(rows, axis=0).astype(BF16)
        return 0
    lax.fori_loop(0, 16, unpack, 0)

    scale = D ** (-0.5)
    keysv[:, HALF:] = (keys_sum[...] * scale).astype(BF16)

    def multiply_zero(b, _):
        block = weight(w.at[0], b)
        for n in range(BLOCK // TOK):
            at = pl.ds(pl.multiple_of(b * BLOCK + n * TOK, 128), TOK)
            part = gnat[at, :TOK] + nt(kgv[:, :HALF], block[n * TOK:(n + 1) * TOK])
            igv[:, at] = (part * scale).astype(BF16)
        return 0
    lax.fori_loop(0, 4, multiply_zero, 0)
    keysv[:, :HALF] = (keys_sum0[...] * scale).astype(BF16)

    for copy in loads[4:]:
        copy.wait()
    other = pl.ds(pl.multiple_of((1 - core) * HALF, 128), HALF)
    got(half_got.at[:, other], o_send.at[2], o_got.at[2])
    half_got[:, mine] = z_got[...]
    outer_grad = half_got[...] * (1.0 / lax.axis_size("rep"))
    momentum_new = outer_mu * ov[...] + outer_grad
    anchor_new = av[...] - outer_rate * (outer_grad + outer_mu * momentum_new)
    momentum_ref[...] = momentum_new
    anchor_ref[...] = anchor_new

    count = jnp.full((1, HALF), step_ref[0].astype(F32), F32)
    fix_first = 1.0 / (1.0 - jnp.exp(count * math.log(beta_first)))
    fix_second = 1.0 / (1.0 - jnp.exp(count * math.log(beta_second)))
    for s in (0, 1):
        at = pl.multiple_of(first_pos[s] * ROWS, 8)
        total = third[s, pl.ds(at, ROWS)]
        for d in (1, 3, 2):
            got(r3.at[s, d], s3_send.at[s, d], s3_got.at[s, d])
            total = total + unpack_rows(r3[s, d])
        gradient = total * scale
        cols = slice(s * HALF, (s + 1) * HALF)
        first_new = beta_first * m1v[:, cols] + (1.0 - beta_first) * gradient
        second_new = beta_second * m2v[:, cols] + (1.0 - beta_second) * gradient * gradient
        direction = first_new * fix_first / (jnp.sqrt(second_new * fix_second) + epsilon)
        local = mv[:, cols]
        stepped = local - inner_rate * (direction + weight_decay * local)
        first_ref[:, cols] = first_new
        second_ref[:, cols] = second_new
        merged_ref[:, cols] = mix_weight * stepped + (1.0 - mix_weight) * anchor_ref[:, cols]

    for copy in pending:
        copy.wait_send()


def exchange(inner_step, *arrays):
    dma = pltpu.SemaphoreType.DMA
    rows = (ROWS, KD)
    return pl.pallas_call(
        kernel,
        out_shape=(
            pltpu.VMEM((TOK, KD), BF16),
            pltpu.VMEM((TOK, D), BF16),
        ) + (pltpu.VMEM(rows, F32),) * 5,
        in_specs=[pl.BlockSpec(memory_space=pl.ANY)] * 8,
        out_specs=(pl.BlockSpec(memory_space=pltpu.VMEM),) * 7,
        scratch_shapes=[
            pltpu.VMEM((TOK, D), BF16),
            pltpu.VMEM((TOK, KD), BF16),
            pltpu.VMEM(rows, F32),
            pltpu.VMEM(rows, F32),
            pltpu.VMEM(rows, F32),
            pltpu.VMEM(rows, F32),
            pltpu.VMEM(rows, F32),
            pltpu.VMEM(rows, F32),
            pltpu.VMEM(rows, F32),
            pltpu.VMEM((ROWS, HALF), F32),
            pltpu.VMEM((ROWS, HALF), F32),
            pltpu.VMEM(rows, F32),
            pltpu.VMEM((2, 16, CHUNK, HALF), BF16),
            pltpu.VMEM((2, 16, CHUNK, HALF), BF16),
            pltpu.VMEM((D, HALF), F32),
            pltpu.VMEM((TOK, HALF), F32),
            pltpu.VMEM((TOK, HALF), F32),
            pltpu.VMEM((TOK, D), BF16),
            pltpu.VMEM((2, 4, 4, 2 * ROWS, HALF // 2), BF16),
            pltpu.VMEM((2, 2, 4, CHUNK, HALF), BF16),
            pltpu.VMEM((2, 2, 2, CHUNK, HALF), BF16),
            pltpu.VMEM((2, 2, 2, HROWS, HALF), BF16),
            pltpu.VMEM((2, 2, HROWS, HALF), BF16),
            pltpu.VMEM((2, CHUNK, HALF), F32),
            pltpu.VMEM((2, 4, 2 * ROWS, HALF // 2), BF16),
            pltpu.VMEM((2, 4, 2 * ROWS, HALF // 2), BF16),
            pltpu.SMEM((1,), jnp.int32),
            dma((8,)), dma((3,)), dma((3,)),
            dma((2, 4)), dma((2, 4)),
            dma((2, 2, 4)), dma((2, 2, 4)), dma((2, 4)), dma((2, 4)),
            dma((2, 2, 4)), dma((2, 2, 4)), dma((2, 4)), dma((2, 4)),
            dma((2, 2, 2, 2)), dma((2, 2, 2, 2)), dma((2, 2, 4)), dma((2, 2, 4)),
            dma((2, 2)), dma((2, 2)), dma((2, 2, 2)), dma((2, 2, 2)), dma((2, 4)), dma((2, 4)),
        ],
        compiler_params=pltpu.CompilerParams(
            collective_id=0, has_side_effects=True, vmem_limit_bytes=56 * 2**20
        ),
        cost_estimate=pl.CostEstimate(
            flops=6 * TOK * D * KD, bytes_accessed=10 * 2**20, transcendentals=0
        ),
        name="exchange",
    )(inner_step, *arrays)


def store_kernel(*refs):
    n = len(refs) // 2
    copies = [pltpu.make_async_copy(refs[i], refs[n + i], refs[-1].at[i]) for i in range(n)]
    for copy in copies:
        copy.start()
    for copy in copies:
        copy.wait()


def store(arrays):
    any_space = pl.BlockSpec(memory_space=pl.ANY)
    return pl.pallas_call(
        store_kernel,
        out_shape=tuple(jax.ShapeDtypeStruct(a.shape, a.dtype) for a in arrays),
        in_specs=[pl.BlockSpec(memory_space=pltpu.VMEM)] * len(arrays),
        out_specs=(any_space,) * len(arrays),
        scratch_shapes=[pltpu.SemaphoreType.DMA((len(arrays),))],
        compiler_params=pltpu.CompilerParams(vmem_limit_bytes=2**20),
        name="store",
    )(*[pltpu.with_memory_space_constraint(a, pltpu.VMEM) for a in arrays])


def body(normed, key_grad, master, first_moment, second_moment, anchor, momentum, inner_step):
    results = exchange(
        inner_step, normed, key_grad, master[0], first_moment[0], second_moment[0], anchor, momentum
    )
    keys, input_grad, merged, first_new, second_new, anchor_new, momentum_new = store(results)
    return (
        keys,
        input_grad,
        merged[None],
        first_new[None],
        second_new[None],
        anchor_new,
        momentum_new,
    )


def solution(mesh):
    in_specs = (
        P(("rep", "fsdp"), None),
        P(("rep", "fsdp"), None),
        P("rep", "fsdp", None),
        P("rep", "fsdp", None),
        P("rep", "fsdp", None),
        P("fsdp", None),
        P("fsdp", None),
        P(),
    )
    out_specs = (
        P(("rep", "fsdp"), None),
        P(("rep", "fsdp"), None),
        P("rep", "fsdp", None),
        P("rep", "fsdp", None),
        P("rep", "fsdp", None),
        P("fsdp", None),
        P("fsdp", None),
    )
    return jax.shard_map(body, mesh=mesh, in_specs=in_specs, out_specs=out_specs, check_vma=False)
```
